256 devices in a mesh: sector: 32 (over z, y_lo, core), axial: 8 (over y_hi, x).
Axes of the slice: x: 4, y: 4 (y_hi: 2, y_lo: 2; y = y_hi * 2 + y_lo), z: 8, core: 2. Of those that a mesh axis runs over, the one named last changes fastest.
Arguments:
- prior_thermal_state: float32 [128, 64, 4096], P('sector', 'axial'), may hold values from -4 to 4
- stepped_thermal_conductance: float32 [128, 64, 4096], P('sector', 'axial'), may hold values from 0.3 to 1
- dissipated_power_input: float32 [128, 64, 4096], P('sector', 'axial'), may hold values from -3 to 3
- substance_label: int32 [128, 64, 4096], P(None, 'axial', 'sector'), may hold values from 0 to 3
- magnet_quality_line: int32 [128, 64, 4096], P(None, 'axial', 'sector'), may hold values from 0 to 3
- permanent_pole_mask: int32 [128, 64, 4096], P(None, 'axial', 'sector'), may hold values 0 or 1
- operator_main_entry: float32 [128, 64, 4096], P(None, 'axial', 'sector'), may hold values from 0.5 to 2
- vector_potential_now: float32 [128, 64, 4096], P(None, 'axial', 'sector'), may hold values from -0.4 to 0.4
- reverse_magnetizing_burden: float32 [128, 64, 4096], P(None, 'axial', 'sector'), may hold values from 0.2 to 5
- inverse_permeability: float32 [4], replicated, may hold values from 0.5 to 4
- remanence_knot_chart: float32 [4, 4], replicated, may hold values from -1 to 2
- coercivity_knot_chart: float32 [4, 4], replicated, may hold values from 0.3 to 2
Outputs:
- relaxed_thermal_state: float32 [128, 64, 4096], P('sector', 'axial')
- updated_potential: float32 [128, 64, 4096], P(None, 'axial', 'sector')
- recursive_misfit: float32 [128, 64, 4096], P(None, 'axial', 'sector')
The draws below stay inside these ranges and needn't reach their ends.
All inputs are finite; a program needn't handle non-finite values. No bound on the sum of `permanent_pole_mask` on one device may be relied on, other than what follows from the above.
Results may differ from the reference program's by a relative error of at most 0.0003.
Values sent between devices are 32-bit elements; how exact they have to be, the bound alone decides.
No kernel may reach another device: no remote copies, remote signals or barrier semaphores. Data moves between devices by JAX's collectives and lax.ppermute only.
A program may use at most 128 MiB of HBM per device.

```python
import math
import jax
import jax.numpy as jnp

SWEEPS = 4
ITERS = 2
MATS = 4
GRADES = 4
KNOTS = 4
SPOKEWISE_SLOTS = 128
LENGTHWISE_SLOTS = 64
ANGULAR_SLOTS = 4096


def draw_vector_potential_now(key, part):
    key = jax.random.fold_in(key, 7)
    beside_all = jnp.arange(ANGULAR_SLOTS, dtype=jnp.float32) / ANGULAR_SLOTS
    scale = 1.0 + 2.0 * beside_all
    values = jax.random.truncated_normal(key, -4.0, 4.0, (SPOKEWISE_SLOTS, LENGTHWISE_SLOTS, ANGULAR_SLOTS), jnp.float32) * scale
    return values * 0.03


def with_ends(values, rng, smallest, high):
    longest = values.shape.index(max(values.shape))
    spots = []
    for shift in (0, 1):
        where = [jax.random.randint(jax.random.fold_in(rng, axis), (), 0, length) for axis, length in enumerate(values.shape)]
        where[longest] = (where[longest] + shift) % values.shape[longest]
        spots.append(tuple(where))
    return values.at[spots[0]].set(smallest).at[spots[1]].set(high)


def levels(rng, shape, cuts, least, top_value):
    factor_of, own = 1.0, jax.random.fold_in(rng, 6)
    for axis_at, shards_of in cuts:
        draws = jnp.exp(jax.random.uniform(jax.random.fold_in(own, axis_at), (shards_of,), jnp.float32, least / len(cuts), top_value / len(cuts)))
        factor_of = factor_of * jnp.repeat(draws, shape[axis_at] // shards_of).reshape([-1 if axis == axis_at else 1 for axis in range(len(shape))])
    return factor_of


def normal_values(key, extent, width, bound, cuts=(), held_as=jnp.bfloat16):
    level = levels(key, extent, cuts, -0.22, 0.18) if cuts else 1.0
    entries = jax.random.normal(key, extent, jnp.float32) * width * level
    return jnp.minimum(jnp.maximum(entries, -bound), bound).astype(held_as)


def setup_inputs(seed: int = 0) -> dict:
    key_of = jax.random.split(jax.random.key(seed), 13)
    prior_thermal_state = normal_values(key_of[0], (SPOKEWISE_SLOTS, LENGTHWISE_SLOTS, ANGULAR_SLOTS), 1.0, 4.0, ((0, 32), (1, 8)), jnp.float32)
    stepped_thermal_conductance = jnp.clip(jnp.exp(math.log(1.0) - 1.2039728 * jax.random.uniform(key_of[1], (SPOKEWISE_SLOTS, LENGTHWISE_SLOTS, ANGULAR_SLOTS), jnp.float32) ** levels(key_of[1], (SPOKEWISE_SLOTS, LENGTHWISE_SLOTS, ANGULAR_SLOTS), ((0, 32), (1, 8)), -0.2, 0.2)), 0.3, 1.0)
    dissipated_power_input = normal_values(key_of[2], (SPOKEWISE_SLOTS, LENGTHWISE_SLOTS, ANGULAR_SLOTS), 0.5, 3.0, ((0, 32), (1, 8)), jnp.float32)
    substance_label = with_ends(jax.random.randint(key_of[3], (SPOKEWISE_SLOTS, LENGTHWISE_SLOTS, ANGULAR_SLOTS), 0, MATS), jax.random.fold_in(key_of[3], 1), 0, MATS - 1).astype(jnp.int32)
    magnet_quality_line = with_ends(jax.random.randint(key_of[4], (SPOKEWISE_SLOTS, LENGTHWISE_SLOTS, ANGULAR_SLOTS), 0, GRADES), jax.random.fold_in(key_of[4], 1), 0, GRADES - 1).astype(jnp.int32)
    permanent_pole_mask = with_ends((jax.random.randint(key_of[5], (SPOKEWISE_SLOTS, LENGTHWISE_SLOTS, ANGULAR_SLOTS), 0, 3) < 1).astype(jnp.int32), jax.random.fold_in(key_of[5], 1), 0, 1)
    operator_main_entry = jnp.clip(jnp.exp(math.log(2.0) - 1.3862944 * jax.random.uniform(key_of[6], (SPOKEWISE_SLOTS, LENGTHWISE_SLOTS, ANGULAR_SLOTS), jnp.float32) ** levels(key_of[6], (SPOKEWISE_SLOTS, LENGTHWISE_SLOTS, ANGULAR_SLOTS), ((1, 8), (2, 32)), -0.2, 0.2)), 0.5, 2.0)
    vector_potential_now = draw_vector_potential_now(jax.random.fold_in(key_of[12], 71), 0)
    reverse_magnetizing_burden = jnp.clip(jnp.exp(math.log(5.0) - 3.218876 * jax.random.uniform(key_of[8], (SPOKEWISE_SLOTS, LENGTHWISE_SLOTS, ANGULAR_SLOTS), jnp.float32) ** levels(key_of[8], (SPOKEWISE_SLOTS, LENGTHWISE_SLOTS, ANGULAR_SLOTS), ((1, 8), (2, 32)), -0.2, 0.2)), 0.2, 5.0)
    inverse_permeability = jnp.clip(jnp.exp(jax.random.uniform(key_of[9], (MATS,), jnp.float32, math.log(0.5), math.log(4.0))), 0.5, 4.0)
    remanence_knot_chart = jnp.clip(jax.random.uniform(key_of[10], (GRADES, KNOTS), jnp.float32, -1.0, 2.0), -1.0, 2.0)
    coercivity_knot_chart = jnp.clip(jax.random.uniform(key_of[11], (GRADES, KNOTS), jnp.float32, 0.3, 2.0), 0.3, 2.0)
    return dict(prior_thermal_state=prior_thermal_state, stepped_thermal_conductance=stepped_thermal_conductance, dissipated_power_input=dissipated_power_input, substance_label=substance_label, magnet_quality_line=magnet_quality_line, permanent_pole_mask=permanent_pole_mask, operator_main_entry=operator_main_entry, vector_potential_now=vector_potential_now, reverse_magnetizing_burden=reverse_magnetizing_burden, inverse_permeability=inverse_permeability, remanence_knot_chart=remanence_knot_chart, coercivity_knot_chart=coercivity_knot_chart)


def sweep(padded_t, padded_k, heat):
    center = padded_t[1:-1, 1:-1]
    kcenter = padded_k[1:-1, 1:-1]
    pairs = [(padded_t[2:, 1:-1], padded_k[2:, 1:-1]), (padded_t[:-2, 1:-1], padded_k[:-2, 1:-1]),
             (padded_t[1:-1, 2:], padded_k[1:-1, 2:]), (padded_t[1:-1, :-2], padded_k[1:-1, :-2]),
             (jnp.roll(center, 1, 2), jnp.roll(kcenter, 1, 2)), (jnp.roll(center, -1, 2), jnp.roll(kcenter, -1, 2))]
    flux = jnp.zeros_like(center)
    for other_t, other_k in pairs:
        flux = flux + 0.5 * (kcenter + other_k) * (other_t - center)
    return center + 0.16 * (flux + heat)


def table_value(table, magnet_quality_line, flux_intensity):
    knots = table.shape[1]
    value = jnp.zeros_like(flux_intensity)
    for col in range(knots):
        coef = jnp.zeros_like(flux_intensity)
        for row in range(table.shape[0]):
            coef = coef + jnp.where(magnet_quality_line == row, table[row, col], 0.0)
        if col == 0:
            value = value + coef
        else:
            value = value + coef * jnp.maximum(flux_intensity - (col - knots // 2), 0.0)
    return value


def magnet_source(flux_intensity, magnet_quality_line, permanent_pole_mask, reverse_magnetizing_burden, remanence_knot_chart, coercivity_knot_chart):
    remanence = table_value(remanence_knot_chart, magnet_quality_line, flux_intensity)
    coercivity = table_value(coercivity_knot_chart, magnet_quality_line, flux_intensity)
    square = coercivity * coercivity
    return permanent_pole_mask.astype(jnp.float32) * remanence * square / (square + reverse_magnetizing_burden)


def reluct_field(substance_label, vector_potential_now, inverse_permeability):
    base = jnp.zeros_like(vector_potential_now)
    for row in range(inverse_permeability.shape[0]):
        base = base + jnp.where(substance_label == row, inverse_permeability[row], 0.0)
    return base * (1.0 + 0.25 * vector_potential_now * vector_potential_now)


def stencil(padded_v, padded_nu, operator_main_entry):
    rows, depth, beside_all = operator_main_entry.shape
    vcenter = padded_v[1:-1, 1:-1, 1:-1]
    ncenter = padded_nu[1:-1, 1:-1, 1:-1]
    total = operator_main_entry * vcenter
    for first in range(3):
        for second in range(3):
            for third in range(3):
                moved = (first != 1) + (second != 1) + (third != 1)
                if moved == 0:
                    continue
                weight = 0.5 ** (moved - 1)
                other_v = padded_v[first:first + rows, second:second + depth, third:third + beside_all]
                other_nu = padded_nu[first:first + rows, second:second + depth, third:third + beside_all]
                total = total + weight * (0.5 * (ncenter + other_nu)) * (vcenter - other_v)
    return total


def pad_global(flux_intensity):
    wrapped = jnp.pad(flux_intensity, ((0, 0), (0, 0), (1, 1)), mode="wrap")
    return jnp.pad(wrapped, ((1, 1), (1, 1), (0, 0)))


def reference(prior_thermal_state, stepped_thermal_conductance, dissipated_power_input, substance_label, magnet_quality_line, permanent_pole_mask, operator_main_entry, vector_potential_now,
              reverse_magnetizing_burden, inverse_permeability, remanence_knot_chart, coercivity_knot_chart):
    padded_k = jnp.pad(stepped_thermal_conductance, ((1, 1), (1, 1), (0, 0)))
    flux_intensity = prior_thermal_state
    for step in range(SWEEPS):
        flux_intensity = sweep(jnp.pad(flux_intensity, ((1, 1), (1, 1), (0, 0))), padded_k, dissipated_power_input)
    relaxed_thermal_state = flux_intensity
    source = magnet_source(flux_intensity, magnet_quality_line, permanent_pole_mask, reverse_magnetizing_burden, remanence_knot_chart, coercivity_knot_chart)
    nu_pad = pad_global(reluct_field(substance_label, vector_potential_now, inverse_permeability))
    recursive_misfit = source - stencil(pad_global(vector_potential_now), nu_pad, operator_main_entry)
    linearized_increment = jnp.zeros_like(vector_potential_now)
    direction = recursive_misfit
    norm_now = jnp.sum(recursive_misfit * recursive_misfit)
    for step in range(ITERS):
        image = stencil(pad_global(direction), nu_pad, operator_main_entry)
        alpha = norm_now / jnp.sum(direction * image)
        linearized_increment = linearized_increment + alpha * direction
        recursive_misfit = recursive_misfit - alpha * image
        if step + 1 < ITERS:
            fresh = jnp.sum(recursive_misfit * recursive_misfit)
            direction = recursive_misfit + (fresh / norm_now) * direction
            norm_now = fresh
    return relaxed_thermal_state, vector_potential_now + linearized_increment, recursive_misfit
```

```python
import jax
import jax.numpy as jnp
from jax import lax
from jax.experimental import pallas as pl
from jax.experimental.pallas import tpu as pltpu
from jax.sharding import PartitionSpec as P

SWEEPS = 4
F32 = jnp.float32
MIB = 1024 * 1024


def call(kernel, out_shapes, args, smem=(), scratch=(), vmem=24, flops=10_000_000):
    specs = [
        pl.BlockSpec(memory_space=pltpu.SMEM if i in smem else pltpu.VMEM)
        for i in range(len(args))
    ]
    moved = sum(a.size * 4 for a in args)
    return pl.pallas_call(
        kernel,
        out_shape=[jax.ShapeDtypeStruct(s, F32) for s in out_shapes],
        in_specs=specs,
        out_specs=[pl.BlockSpec(memory_space=pltpu.VMEM)] * len(out_shapes),
        scratch_shapes=list(scratch),
        compiler_params=pltpu.CompilerParams(vmem_limit_bytes=vmem * MIB),
        cost_estimate=pl.CostEstimate(flops=flops, bytes_accessed=moved, transcendentals=0),
    )(*args)


def roll(x, shift, axis):
    return pltpu.roll(x, shift % x.shape[axis], axis)


def iota(shape, axis):
    return lax.broadcasted_iota(jnp.int32, shape, axis)


def beside(x, low, high):
    place = iota(x.shape, 0)
    depth = x.shape[0]
    minus = jnp.where(place == 0, low, roll(x, 1, 0))
    plus = jnp.where(place == depth - 1, high, roll(x, -1, 0))
    return minus, plus


def conduct_kernel(k, k_up, k_down, k_low, k_high, radial, around, minus, plus):
    rows = k.shape[0]
    for r in range(rows):
        own = k[r]
        above = k_up[0] if r == 0 else k[r - 1]
        radial[r] = 0.08 * (own + above)
        around[r] = 0.08 * (own + roll(own, -1, 1))
        low, high = beside(own, k_low[r : r + 1], k_high[r : r + 1])
        minus[r] = 0.08 * (own + low)
        plus[r] = 0.08 * (own + high)
    radial[rows] = 0.08 * (k[rows - 1] + k_down[0])


def sweep_kernel(
    last, u, u_up, u_down, u_low, u_high, heat, radial, around, minus, plus, *outs
):
    rows, depth, width = u.shape
    for r in range(rows):
        own = u[r]
        above = u_up[0] if r == 0 else u[r - 1]
        below = u_down[0] if r == rows - 1 else u[r + 1]
        flow = around[r] * (roll(own, -1, 1) - own)
        low, high = beside(own, u_low[r : r + 1], u_high[r : r + 1])
        new = own + (
            (flow - roll(flow, 1, 1))
            + (radial[r] * (above - own) + radial[r + 1] * (below - own))
            + (minus[r] * (low - own) + plus[r] * (high - own))
            + 0.16 * heat[r]
        )
        outs[0][r] = new
        if last:
            for j in range(width // 128):
                outs[1][j, r] = new[:, 128 * j : 128 * j + 128]
        else:
            outs[1][r : r + 1] = new[0:1]
            outs[2][r : r + 1] = new[depth - 1 : depth]


def packed_pair(tile_of, rows, width, col):
    lane = iota((8, width), 1)
    half = width // 2
    out = []
    for t in range(rows // half):
        acc = jnp.zeros((8, width), F32)
        for i in range(half):
            acc = jnp.where(lane // 2 == i, tile_of(half * t + i, 2 * i - col), acc)
        out.append(acc)
    return out


def prep_kernel(v, label, diag, table, nu, pack_up, pack_down):
    rows, _, width = v.shape

    def body(r, _):
        kind = label[r]
        base = jnp.full(kind.shape, table[0], F32)
        for m in range(1, table.shape[0]):
            base = jnp.where(kind == m, table[m], base)
        here = v[r]
        nu[r] = base * (1.0 + 0.25 * here * here)
        return 0

    lax.fori_loop(0, rows, body, 0, unroll=8)
    lane = iota((8, width), 1)
    even = lane % 2 == 0
    for pack, nu_col, col in ((pack_up, width - 2, width - 1), (pack_down, 0, 0)):
        pairs = packed_pair(lambda r, s: roll(nu[r], s, 1), rows, width, nu_col)
        mixed = packed_pair(
            lambda r, s: jnp.where(even, roll(v[r], s, 1), roll(diag[r], s + 1, 1)),
            rows,
            width,
            col,
        )
        for t, tile in enumerate(pairs + mixed):
            pack[t] = tile


def edges_kernel(nu, v, diag, from_low, from_high, up, down):
    rows, depth, _ = nu.shape
    up[0:rows] = nu[:, depth - 2 : depth, :]
    down[0:rows] = nu[:, 0:2, :]
    up[rows : 2 * rows, 0:1] = v[:, depth - 1 : depth, :]
    up[rows : 2 * rows, 1:2] = diag[:, depth - 1 : depth, :]
    down[rows : 2 * rows, 0:1] = v[:, 0:1, :]
    down[rows : 2 * rows, 1:2] = diag[:, 0:1, :]
    for j, ref in ((0, from_low), (4, from_high)):
        up[2 * rows + j : 2 * rows + j + 4] = ref[:, depth - 2 : depth, :]
        down[2 * rows + j : 2 * rows + j + 4] = ref[:, 0:2, :]


def tall_tile(own, high, low):
    width = own.shape[1]
    empty = jnp.zeros((4, width), F32)
    return jnp.concatenate([own, high, empty, low], axis=0)


def blur(x):
    x = x + 0.5 * (roll(x, 1, 1) + roll(x, -1, 1))
    return x + 0.5 * (roll(x, 1, 0) + roll(x, -1, 0))


def setup_kernel(
    v, nu, diag, from_low, from_high, ax_low, ax_high, nu_ext, main, load, v_ext, one, two
):
    rows, depth, width = v.shape
    half = width // 2
    lane = iota((2 * depth, width), 1)
    sides = []
    for j, ref in ((0, from_low), (4, from_high)):
        sides.append(
            [
                tall_tile(ref[t], ax_high[2 * rows + j + t], ax_low[2 * rows + j + t])
                for t in range(2 * (rows // half))
            ]
        )
    lows, highs = sides
    own = slice(0, depth)
    for t in range(rows // half):

        def fill(i, _):
            r = half * t + i
            nu_ext[r, own, 0:width] = nu[r]
            v_ext[r, own, 0:width] = v[r]
            main[r, own, 0:width] = diag[r]
            empty = jnp.zeros((depth - 4, width), F32)
            one_row = jnp.zeros((depth - 2, width), F32)
            nu_ext[r, depth : 2 * depth, 0:width] = jnp.concatenate(
                [ax_high[r], empty, ax_low[r]], axis=0
            )
            mixed_high, mixed_low = ax_high[rows + r], ax_low[rows + r]
            v_ext[r, depth : 2 * depth, 0:width] = jnp.concatenate(
                [mixed_high[0:1], one_row, mixed_low[0:1]], axis=0
            )
            main[r, depth : 2 * depth, 0:width] = jnp.concatenate(
                [mixed_high[1:2], one_row, mixed_low[1:2]], axis=0
            )

            def lanes(low, high, low_at, high_at, count):
                return jnp.where(
                    lane < count,
                    pltpu.roll(high, (width + high_at - 2 * i) % width, 1),
                    jnp.where(
                        lane >= width - count,
                        pltpu.roll(low, (2 * width + low_at - 2 * i) % width, 1),
                        0.0,
                    ),
                )

            n = rows // half
            nu_ext[r, :, width : 2 * width] = lanes(lows[t], highs[t], width - 2, 0, 2)
            v_ext[r, :, width : 2 * width] = lanes(lows[n + t], highs[n + t], width - 1, 0, 1)
            main[r, :, width : 2 * width] = lanes(
                lows[n + t], highs[n + t], width - 2, width - 1, 1
            )
            return 0

        lax.fori_loop(0, half, fill, 0, unroll=4)

    zero = jnp.zeros((2 * depth, 2 * width), F32)
    one[0] = zero
    one[rows + 1] = zero
    two[0] = zero
    two[rows + 1] = zero

    def first(r, _):
        one[r + 1] = blur(nu_ext[r])
        return 0

    lax.fori_loop(0, rows, first, 0, unroll=2)

    def second(r, _):
        n = nu_ext[r]
        main[r] = main[r] + 8.0 * n + (one[r + 1] + 0.5 * (one[r] + one[r + 2]))
        return 0

    lax.fori_loop(0, rows, second, 0, unroll=2)

    def third(r, _):
        x = v_ext[r]
        one[r + 1] = blur(x)
        two[r + 1] = blur(x * nu_ext[r])
        return 0

    lax.fori_loop(0, rows, third, 0, unroll=2)

    def fourth(r, _):
        load[r] = applied(r, v_ext, nu_ext, main, one, two, own, slice(0, width))
        return 0

    lax.fori_loop(0, rows, fourth, 0, unroll=2)


def applied(r, x, nu, main, one, two, places, lanes):
    at = (places, lanes)
    near = one[(r + 1, *at)] + 0.5 * (one[(r, *at)] + one[(r + 2, *at)])
    weighed = two[(r + 1, *at)] + 0.5 * (two[(r, *at)] + two[(r + 2, *at)])
    return main[(r, *at)] * x[(r, *at)] - nu[(r, *at)] * near - weighed


def residual_kernel(t, grade, mask, burden, load, rem, coer, res, pack_up, pack_down):
    rows, _, width = t.shape
    grades, knots = rem.shape

    def body(r, _):
        which = grade[r]
        here = t[r]
        chosen = [which == g for g in range(grades)]

        def value(table):
            total = None
            for col in range(knots):
                coef = jnp.full(here.shape, table[0, col], F32)
                for g in range(1, grades):
                    coef = jnp.where(chosen[g], table[g, col], coef)
                if col:
                    coef = total + coef * jnp.maximum(here - (col - knots // 2), 0.0)
                total = coef
            return total

        remanence = value(rem)
        coercivity = value(coer)
        square = coercivity * coercivity
        source = mask[r].astype(F32) * remanence * square / (square + burden[r])
        res[r] = source - load[r]
        return 0

    lax.fori_loop(0, rows, body, 0, unroll=4)
    for pack, col in ((pack_up, width - 2), (pack_down, 0)):
        for i, tile in enumerate(
            packed_pair(lambda r, s: roll(res[r], s, 1), rows, width, col)
        ):
            pack[i] = tile


def res_edges_kernel(res, from_low, from_high, up, down):
    rows, depth, _ = res.shape
    up[0:rows] = res[:, depth - 2 : depth, :]
    down[0:rows] = res[:, 0:2, :]
    for j, ref in ((0, from_low), (2, from_high)):
        up[rows + j : rows + j + 2] = ref[:, depth - 2 : depth, :]
        down[rows + j : rows + j + 2] = ref[:, 0:2, :]


def gram_kernel(
    res, from_low, from_high, ax_low, ax_high, nu, main, q, kq, sums, x_ext, q_ext, one, two
):
    rows, depth, width = res.shape
    half = width // 2
    lane = iota((2 * depth, width), 1)
    lows, highs = [
        [
            tall_tile(ref[t], ax_high[rows + j + t], ax_low[rows + j + t])
            for t in range(rows // half)
        ]
        for j, ref in ((0, from_low), (2, from_high))
    ]
    zero = jnp.zeros((2 * depth, 2 * width), F32)
    for ref in (one, two):
        ref[0] = zero
        ref[rows + 1] = zero
    for t in range(rows // half):

        def fill(i, _):
            r = half * t + i
            empty = jnp.zeros((depth - 4, width), F32)
            x_ext[r, 0:depth, 0:width] = res[r]
            x_ext[r, depth : 2 * depth, 0:width] = jnp.concatenate(
                [ax_high[r], empty, ax_low[r]], axis=0
            )
            x_ext[r, :, width : 2 * width] = jnp.where(
                lane < 2,
                pltpu.roll(highs[t], (width - 2 * i) % width, 1),
                jnp.where(
                    lane >= width - 2,
                    pltpu.roll(lows[t], (2 * width - 2 - 2 * i) % width, 1),
                    0.0,
                ),
            )
            x = x_ext[r]
            one[r + 1] = blur(x)
            two[r + 1] = blur(x * nu[r])
            return 0

        lax.fori_loop(0, half, fill, 0, unroll=2)

    slab = lax.axis_index("axial")
    place = iota((2 * depth, 2 * width), 0)
    outside = jnp.logical_or(
        jnp.logical_and(place >= 2 * depth - 4, slab == 0),
        jnp.logical_and(
            jnp.logical_and(place >= depth, place < depth + 4),
            slab == lax.axis_size("axial") - 1,
        ),
    )
    whole = (slice(None), slice(None))
    own = (slice(0, depth), slice(0, width))

    def image(r, carry):
        a, b, c = carry
        y = applied(r, x_ext, nu, main, one, two, *whole)
        y = jnp.where(outside, 0.0, y)
        q_ext[r] = y
        y = y[0:depth, 0:width]
        q[r] = y
        x = res[r]
        return a + x * x, b + x * y, c + y * y

    none = jnp.zeros((depth, width), F32)
    a, b, c = lax.fori_loop(0, rows, image, (none, none, none), unroll=2)

    def third(r, _):
        x = q_ext[r]
        one[r + 1] = blur(x)
        two[r + 1] = blur(x * nu[r])
        return 0

    lax.fori_loop(0, rows, third, 0, unroll=2)

    def again(r, d):
        y = applied(r, q_ext, nu, main, one, two, *own)
        kq[r] = y
        return d + y * q[r]

    d = lax.fori_loop(0, rows, again, none, unroll=2)
    spot = iota((1, width), 1)
    line = jnp.zeros((1, width), F32)
    for i, part in enumerate((a, b, c, d)):
        line = jnp.where(spot == i, jnp.sum(part), line)
    for j in range(sums.shape[0]):
        sums[j] = line


def final_kernel(parts, v, res, q, kq, potential, misfit):
    rows = v.shape[0]
    total = parts[0]
    for j in range(1, parts.shape[0]):
        total = total + parts[j]
    rr, rq, qq, qk = [total[0:1, i : i + 1] for i in range(4)]
    alpha = rr / rq
    fresh = alpha * alpha * qq - 2.0 * alpha * rq + rr
    ratio = 1.0 + fresh / rr
    bend = ratio * ratio * rq - 2.0 * alpha * ratio * qq + alpha * alpha * qk
    again = fresh / bend
    straight = alpha + again * ratio
    cross = again * alpha
    straight = jnp.broadcast_to(straight, v.shape[1:])
    cross = jnp.broadcast_to(cross, v.shape[1:])

    def body(r, _):
        x, y = res[r], q[r]
        potential[r] = v[r] + (straight * x - cross * y)
        misfit[r] = x - straight * y + cross * kq[r]
        return 0

    lax.fori_loop(0, rows, body, 0, unroll=8)


def shifted(x, axis, step, wrap):
    n = lax.axis_size(axis)
    pairs = [(i, (i + step) % n) for i in range(n) if wrap or 0 <= i + step < n]
    return lax.ppermute(x, axis, pairs)


def both_ways(up, down, axis, wrap):
    return shifted(up, axis, 1, wrap), shifted(down, axis, -1, wrap)


def local(
    prior_thermal_state,
    stepped_thermal_conductance,
    dissipated_power_input,
    substance_label,
    magnet_quality_line,
    permanent_pole_mask,
    operator_main_entry,
    vector_potential_now,
    reverse_magnetizing_burden,
    inverse_permeability,
    remanence_knot_chart,
    coercivity_knot_chart,
):
    u, k, heat = prior_thermal_state, stepped_thermal_conductance, dissipated_power_input
    v, diag = vector_potential_now, operator_main_entry
    thick, depth, around = u.shape
    rows, _, width = v.shape
    block = (rows, depth, width)
    wide = (rows, 2 * depth, 2 * width)
    scratch_wide = pltpu.VMEM(wide, F32)
    scratch_tall = pltpu.VMEM((rows + 2, 2 * depth, 2 * width), F32)
    tiles = rows * 2 // width
    sectors = lax.axis_size("sector")

    k_up, k_down = both_ways(k[thick - 1 :], k[:1], "sector", False)
    k_low, k_high = both_ways(k[:, depth - 1], k[:, 0], "axial", False)
    faces = (thick + 1, depth, around)
    planes = call(
        conduct_kernel, [faces, u.shape, u.shape, u.shape], [k, k_up, k_down, k_low, k_high]
    )
    nu, pack_up, pack_down = call(
        prep_kernel,
        [block, (2 * tiles, depth, width), (2 * tiles, depth, width)],
        [v, substance_label, diag, inverse_permeability],
        smem=(3,),
    )
    first, last = u[:, 0], u[:, depth - 1]
    for step in range(SWEEPS):
        u_up, u_down = both_ways(u[thick - 1 :], u[:1], "sector", False)
        u_low, u_high = both_ways(last, first, "axial", False)
        final = step + 1 == SWEEPS
        edge = (thick, around)
        outs = (
            [u.shape, (sectors, thick, depth, width)] if final else [u.shape, edge, edge]
        )
        made = call(
            lambda *refs, final=final: sweep_kernel(final, *refs),
            outs,
            [u, u_up, u_down, u_low, u_high, heat, *planes],
        )
        if final:
            u, cut = made
        else:
            u, first, last = made
        if step == 0:
            from_low, from_high = both_ways(pack_up, pack_down, "sector", True)
            spread = (2 * rows + 8 * tiles // 2, 2, width)
            up, down = call(
                edges_kernel, [spread, spread], [nu, v, diag, from_low, from_high]
            )
        if step == 1:
            ax_low, ax_high = both_ways(up, down, "axial", False)
            nu_ext, main, load = call(
                setup_kernel,
                [wide, wide, block],
                [v, nu, diag, from_low, from_high, ax_low, ax_high],
                scratch=[scratch_wide, scratch_tall, scratch_tall],
                vmem=40,
            )
    sector_field = lax.all_to_all(cut, "sector", 0, 0).reshape(block)
    pair = (tiles, depth, width)
    res, pack_up, pack_down = call(
        residual_kernel,
        [block, pair, pair],
        [
            sector_field,
            magnet_quality_line,
            permanent_pole_mask,
            reverse_magnetizing_burden,
            load,
            remanence_knot_chart,
            coercivity_knot_chart,
        ],
        smem=(5, 6),
    )
    from_low, from_high = both_ways(pack_up, pack_down, "sector", True)
    spread = (rows + 2 * tiles, 2, width)
    up, down = call(res_edges_kernel, [spread, spread], [res, from_low, from_high])
    ax_low, ax_high = both_ways(up, down, "axial", False)
    q, kq, sums = call(
        gram_kernel,
        [block, block, (sectors, 1, width)],
        [res, from_low, from_high, ax_low, ax_high, nu_ext, main],
        scratch=[scratch_wide, scratch_wide, scratch_tall, scratch_tall],
        vmem=40,
    )
    slabs = lax.axis_size("axial")
    sums = jnp.sum(lax.all_to_all(sums, "sector", 0, 0), axis=0)
    sums = lax.all_to_all(jnp.broadcast_to(sums[None], (slabs, 1, width)), "axial", 0, 0)
    potential, misfit = call(final_kernel, [block, block], [sums, v, res, q, kq])
    return u, potential, misfit


def solution(mesh):
    thermal = P("sector", "axial", None)
    magnetic = P(None, "axial", "sector")
    return jax.shard_map(
        local,
        mesh=mesh,
        in_specs=(thermal,) * 3 + (magnetic,) * 6 + (P(),) * 3,
        out_specs=(thermal, magnetic, magnetic),
        check_vma=False,
    )
```

```python
import jax
import jax.numpy as jnp
from jax import lax
from jax.experimental import pallas as pl
from jax.experimental.pallas import tpu as pltpu
from jax.sharding import PartitionSpec as P

SWEEPS = 4
SECTOR = ("chip", "core")
AXIAL = "axial"
F32 = jnp.float32
MIB = 1024 * 1024


def call(kernel, out_shapes, args, smem=(), hbm=(), scratch=(), vmem=14, flops=10_000_000):
    spaces = [
        pltpu.SMEM if i in smem else pl.ANY if i in hbm else pltpu.VMEM
        for i in range(len(args))
    ]
    specs = [pl.BlockSpec(memory_space=space) for space in spaces]
    moved = sum(a.size * 4 for a in args)
    return pl.pallas_call(
        kernel,
        out_shape=[jax.ShapeDtypeStruct(s, F32) for s in out_shapes],
        in_specs=specs,
        out_specs=[pl.BlockSpec(memory_space=pltpu.VMEM)] * len(out_shapes),
        scratch_shapes=list(scratch),
        compiler_params=pltpu.CompilerParams(vmem_limit_bytes=vmem * MIB),
        cost_estimate=pl.CostEstimate(flops=flops, bytes_accessed=moved, transcendentals=0),
    )(*args)


def roll(x, shift, axis):
    return pltpu.roll(x, shift % x.shape[axis], axis)


def iota(shape, axis):
    return lax.broadcasted_iota(jnp.int32, shape, axis)


def place_on(axis):
    if isinstance(axis, str):
        return lax.axis_index(axis), lax.axis_size(axis)
    major, minor = axis
    size = lax.axis_size(minor)
    return lax.axis_index(major) * size + lax.axis_index(minor), lax.axis_size(major) * size


def is_even(axis):
    return place_on(axis)[0] % 2 == 0


def by_parity(even, a, b):
    return jnp.where(even, a, b), jnp.where(even, b, a)


def swapped(a, b, axis):
    if axis == SECTOR:
        n = lax.axis_size("chip") * lax.axis_size("core")
        first = [(i, i ^ 1) for i in range(n)]
        second = [(i, (i + 1) % n if i % 2 else (i - 1) % n) for i in range(n)]
        return lax.ppermute(a, SECTOR, first), lax.ppermute(b, SECTOR, second)
    n = lax.axis_size(AXIAL)
    first = [(i, i ^ 1) for i in range(n)]
    second = []
    for s in range(lax.axis_size("chip") * lax.axis_size("core")):
        for i in range(n):
            if 0 < i < n - 1:
                second.append((s * n + i, s * n + (i + 1 if i % 2 else i - 1)))
            else:
                second.append((s * n + i, (s ^ 1) * n + i))
    b = lax.ppermute(b, (*SECTOR, AXIAL), second)
    return lax.ppermute(a, AXIAL, first), b


def thermal_swaps(row_a, row_b, edge_a, edge_b):
    edges = swapped(edge_a, edge_b, AXIAL)
    return [*swapped(row_a, row_b, SECTOR), *edges]


def inner(axis):
    place, size = place_on(axis)
    return place > 0, place < size - 1


def thermal_edges_kernel(u, k, row_a, row_b, edge_a, edge_b):
    rows, depth, _ = u.shape
    even, even_slab = is_even(SECTOR), is_even(AXIAL)
    for i, x in enumerate((u, k)):
        row_a[i], row_b[i] = by_parity(even, x[rows - 1], x[0])
        for r in range(rows):
            at = slice(i * rows + r, i * rows + r + 1)
            edge_a[at], edge_b[at] = by_parity(even_slab, x[r, depth - 1 : depth], x[r, 0:1])


def beside(x, low, high):
    place = iota(x.shape, 0)
    depth = x.shape[0]
    minus = jnp.where(place == 0, low, roll(x, 1, 0))
    plus = jnp.where(place == depth - 1, high, roll(x, -1, 0))
    return minus, plus


def conduct(k, edges, radial, around, minus, plus):
    k_up, k_down, k_low, k_high = edges
    rows = k.shape[0]
    for r in range(rows):
        own = k[r]
        above = k_up if r == 0 else k[r - 1]
        radial[r] = 0.08 * (own + above)
        around[r] = 0.08 * (own + roll(own, -1, 1))
        low, high = beside(own, k_low[r], k_high[r])
        minus[r] = 0.08 * (own + low)
        plus[r] = 0.08 * (own + high)
    radial[rows] = 0.08 * (k[rows - 1] + k_down)


def edges_of(refs, which, rows, width):
    row_a, row_b, edge_a, edge_b = refs
    above, below = inner(SECTOR)
    before, after = inner(AXIAL)
    even_slab = is_even(AXIAL)
    down, up = by_parity(is_even(SECTOR), row_a[which, :, 0:width], row_b[which, :, 0:width])
    lows, highs = [], []
    for i in range(which * rows, which * rows + rows):
        high, low = by_parity(even_slab, edge_a[i : i + 1], edge_b[i : i + 1])
        lows.append(jnp.where(before, low, 0.0))
        highs.append(jnp.where(after, high, 0.0))
    return jnp.where(above, up, 0.0), jnp.where(below, down, 0.0), lows, highs


def sweep(u, edges, heat, radial, around, minus, plus):
    u_up, u_down, u_low, u_high = edges
    rows = u.shape[0]
    for r in range(rows):
        own = u[r]
        above = u_up if r == 0 else u[r - 1]
        below = u_down if r == rows - 1 else u[r + 1]
        flow = around[r] * (roll(own, -1, 1) - own)
        low, high = beside(own, u_low[r], u_high[r])
        yield r, own + (
            (flow - roll(flow, 1, 1))
            + (radial[r] * (above - own) + radial[r + 1] * (below - own))
            + (minus[r] * (low - own) + plus[r] * (high - own))
            + 0.16 * heat[r]
        )


def keep_edge(swept, out, edge_b):
    even_slab = is_even(AXIAL)
    for r, new in swept:
        depth = new.shape[0]
        out[r] = new
        edge_b[r : r + 1] = by_parity(even_slab, new[depth - 1 : depth], new[0:1])[1]


def rest_kernel(u, *refs):
    *packs, row_a, row_b, edge_a = refs
    rows, depth, width = u.shape
    even_slab = is_even(AXIAL)
    row_a[0, :, 0:width], row_b[0, :, 0:width] = by_parity(
        is_even(SECTOR), u[rows - 1], u[0]
    )
    for r in range(rows):
        edge_a[r : r + 1] = by_parity(even_slab, u[r, depth - 1 : depth], u[r, 0:1])[0]
    for out, pack in zip((row_a, row_b), packs):
        for i in range(2):
            lanes = pack.shape[2]
            out[0, :, width + i * lanes : width + (i + 1) * lanes] = pack[i]


def first_sweep_kernel(u, k, row_a, row_b, edge_a, edge_b, heat, out, edge_out, *planes):
    refs = (row_a, row_b, edge_a, edge_b)
    rows, _, width = u.shape
    conduct(k, edges_of(refs, 1, rows, width), *planes)
    keep_edge(sweep(u, edges_of(refs, 0, rows, width), heat, *planes), out, edge_out)


def sweep_kernel(u, row_a, row_b, edge_a, edge_b, heat, *rest):
    planes, (out, edge_out) = rest[:4], rest[4:]
    rows, _, width = u.shape
    edges = edges_of((row_a, row_b, edge_a, edge_b), 0, rows, width)
    keep_edge(sweep(u, edges, heat, *planes), out, edge_out)


def last_sweep_kernel(u, row_a, row_b, edge_a, edge_b, heat, *rest):
    planes, cut = rest[:4], rest[-1]
    rows, _, width = u.shape
    edges = edges_of((row_a, row_b, edge_a, edge_b), 0, rows, width)
    for r, new in sweep(u, edges, heat, *planes):
        for j in range(new.shape[1] // 128):
            cut[j, r] = new[:, 128 * j : 128 * j + 128]


def whole_kernel(cut, out):
    for r in range(out.shape[0]):
        for j in range(cut.shape[0]):
            out[r, :, 128 * j : 128 * j + 128] = cut[j, r]


def packed(tile_of, rows, width, col):
    lane = iota((8, width), 1)
    half = width // 2
    out = []
    for t in range(rows // half):
        acc = jnp.zeros((8, width), F32)
        for i in range(half):
            acc = jnp.where(lane // 2 == i, tile_of(half * t + i, 2 * i - col), acc)
        out.append(acc)
    return jnp.concatenate(out, axis=1)


def prep_kernel(v, label, diag, table, nu, pack_a, pack_b):
    rows, _, width = v.shape

    def body(r, _):
        kind = label[r]
        base = jnp.full(kind.shape, table[0], F32)
        for m in range(1, table.shape[0]):
            base = jnp.where(kind == m, table[m], base)
        here = v[r]
        nu[r] = base * (1.0 + 0.25 * here * here)
        return 0

    lax.fori_loop(0, rows, body, 0, unroll=16)
    even = iota((8, width), 1) % 2 == 0
    made = []
    for nu_col, col in ((width - 2, width - 1), (0, 0)):
        pairs = packed(lambda r, s: roll(nu[r], s, 1), rows, width, nu_col)
        mixed = packed(
            lambda r, s: jnp.where(even, roll(v[r], s, 1), roll(diag[r], s + 1, 1)),
            rows,
            width,
            col,
        )
        made.append((pairs, mixed))
    for i in range(2):
        pack_a[i], pack_b[i] = by_parity(is_even(SECTOR), made[0][i], made[1][i])


def put_packs(packs, at, even, out_a, out_b):
    for pack in packs:
        depth, lanes = pack.shape
        for j in range(lanes // 128):
            cut = pack[:, 128 * j : 128 * j + 128]
            out_a[at], out_b[at] = by_parity(even, cut[depth - 2 : depth], cut[0:2])
            at += 1


def put_edges(field, at, even, out_a, out_b):
    rows, depth, _ = field.shape
    out_a[at : at + rows], out_b[at : at + rows] = by_parity(
        even, field[:, depth - 2 : depth, :], field[:, 0:2, :]
    )


def static_packs(own_a, own_b, row_a, row_b):
    even = is_even(SECTOR)
    lanes = own_a.shape[2]
    width = row_a.shape[2] - 2 * lanes
    own_up, own_down = by_parity(even, own_a[0], own_b[0])
    spans = [slice(width + i * lanes, width + (i + 1) * lanes) for i in range(2)]
    nu_high, nu_low = by_parity(even, row_a[0, :, spans[0]], row_b[0, :, spans[0]])
    mix_high, mix_low = by_parity(even, row_a[0, :, spans[1]], row_b[0, :, spans[1]])
    return [nu_low, nu_high, own_down, own_up, mix_low, mix_high]


def edges_kernel(nu, v, diag, own_a, own_b, row_a, row_b, out_a, out_b):
    rows, depth, _ = nu.shape
    even = is_even(AXIAL)
    put_edges(nu, 0, even, out_a, out_b)
    for i, field in enumerate((v, diag)):
        out_a[rows : 2 * rows, i : i + 1], out_b[rows : 2 * rows, i : i + 1] = by_parity(
            even, field[:, depth - 1 : depth, :], field[:, 0:1, :]
        )
    put_packs(static_packs(own_a, own_b, row_a, row_b), 2 * rows, even, out_a, out_b)


def residual_packs(own_a, own_b, got_a, got_b):
    even = is_even(SECTOR)
    up, down = by_parity(even, own_a[...], own_b[...])
    high, low = by_parity(even, got_a[...], got_b[...])
    return [low, high, down, up]


def residual_edges_kernel(res, own_a, own_b, got_a, got_b, out_a, out_b):
    even = is_even(AXIAL)
    put_edges(res, 0, even, out_a, out_b)
    put_packs(residual_packs(own_a, own_b, got_a, got_b), res.shape[0], even, out_a, out_b)


def tall(own, high, low):
    empty = jnp.zeros((own.shape[0] - 4, own.shape[1]), F32)
    return jnp.concatenate([own, high, empty, low], axis=0)


def beyond(ax_a, ax_b, at):
    before, after = inner(AXIAL)
    high, low = by_parity(is_even(AXIAL), ax_a[at], ax_b[at])
    return jnp.where(after, high, 0.0), jnp.where(before, low, 0.0)


def tall_packs(packs, at, ax_a, ax_b):
    out = []
    for pack in packs:
        span = range(at, at + pack.shape[1] // 128)
        pairs = [beyond(ax_a, ax_b, j) for j in span]
        high, low = [jnp.concatenate(parts, axis=1) for parts in zip(*pairs)]
        out.append(tall(pack, high, low))
        at = span.stop
    return out


def side_of(low, high):
    return jnp.where(iota(low.shape, 1) % 2 == 1, low, high)


def axial_blur(x):
    return x + 0.5 * (roll(x, 1, 0) + roll(x, -1, 0))


def radial_blur_side(x):
    lane = iota(x.shape, 1)
    lanes = x.shape[1]
    above = jnp.where(lane < 2, 0.0, roll(x, 2, 1))
    below = jnp.where(lane >= lanes - 2, 0.0, roll(x, -2, 1))
    return x + 0.5 * (above + below)


def blur_side(low, high, down, up):
    left = low + 0.5 * roll(low + down, 1, 1)
    right = high + 0.5 * roll(high + up, -1, 1)
    return radial_blur_side(axial_blur(side_of(left, right)))


def around_blur(x, side):
    lane = iota(x.shape, 1)
    width = x.shape[1]
    before = jnp.where(lane == 0, side, roll(x, 1, 1))
    after = jnp.where(lane == width - 1, side, roll(x, -1, 1))
    return x + 0.5 * (before + after)


def radial_blur(ref, r):
    return ref[r + 1] + 0.5 * (ref[r] + ref[r + 2])


def clear_ends(*refs):
    for ref in refs:
        zero = jnp.zeros(ref.shape[1:], F32)
        ref[0] = zero
        ref[ref.shape[0] - 1] = zero


def by_half(rows, width, body, carry, unroll):
    half = width // 2
    for t in range(rows // half):

        def step(i, c, t=t):
            return body(half * t + i, t, (2 * width - 1 - 2 * i) % width, c)

        carry = lax.fori_loop(0, half, step, carry, unroll=unroll)
    return carry


def tile(ref, t, depth):
    return ref[0:depth, 128 * t : 128 * t + 128]


def setup_kernel(
    v, nu, diag, grade, mask, burden, own_a, own_b, row_a, row_b, ax_a, ax_b,
    nu_tall, main, ready, packs, main_side, v_tall, p_tall, blurred
):
    rows, depth, width = v.shape
    nu_low, nu_high, nu_down, nu_up, mix_low, mix_high = tall_packs(
        static_packs(own_a, own_b, row_a, row_b), 2 * rows, ax_a, ax_b
    )
    odd = iota(mix_low.shape, 1) % 2 == 1
    v_side = jnp.where(odd, roll(mix_low, 1, 1), mix_high)
    diag_side = jnp.where(odd, mix_low, roll(mix_high, -1, 1))
    nu_side = side_of(nu_low, nu_high)
    for i, pack in enumerate((nu_low, nu_high, nu_down, nu_up)):
        packs[i] = pack
    main_side[...] = diag_side + 8.0 * nu_side + blur_side(nu_low, nu_high, nu_down, nu_up)
    for i, side in enumerate((nu_side, v_side, v_side * nu_side)):
        blurred[i] = radial_blur_side(axial_blur(side))
    clear_ends(nu_tall, v_tall, p_tall)

    def fill(r, _):
        mixed_high, mixed_low = beyond(ax_a, ax_b, rows + r)
        n = tall(nu[r], *beyond(ax_a, ax_b, r))
        empty = jnp.zeros((depth - 2, width), F32)
        x = jnp.concatenate([v[r], mixed_high[0:1], empty, mixed_low[0:1]], axis=0)
        nu_tall[r + 1] = n
        v_tall[r + 1] = x
        p_tall[r + 1] = x * n
        ready[0, r] = jnp.where(mask[r] == 1, grade[r], -1).astype(F32)
        ready[1, r] = burden[r]
        main[r] = jnp.concatenate([diag[r], mixed_high[1:2], empty, mixed_low[1:2]], axis=0)
        return 0

    lax.fori_loop(0, rows, fill, 0, unroll=16)

    def body(r, t, shift, _):
        n = nu_tall[r + 1]
        side = pltpu.roll(tile(blurred.at[0], t, 2 * depth), shift, 1)
        field = around_blur(axial_blur(radial_blur(nu_tall, r)), side)
        whole = main[r] + 8.0 * n + field
        main[r] = whole
        near, weighed = [
            around_blur(
                axial_blur(radial_blur(ref, r))[0:depth],
                pltpu.roll(tile(blurred.at[i], t, depth), shift, 1),
            )
            for i, ref in ((1, v_tall), (2, p_tall))
        ]
        ready[2, r] = whole[0:depth] * v[r] - n[0:depth] * near - weighed
        return 0

    by_half(rows, width, body, 0, 16)


def residual_kernel(t, ready, rem, coer, res, pack_a, pack_b):
    rows, _, width = t.shape
    grades, knots = rem.shape

    def body(r, _):
        which = ready[0, r]
        here = t[r]
        chosen = [which == g for g in range(grades)]
        ramps = [jnp.maximum(here - (col - knots // 2), 0.0) for col in range(1, knots)]

        def value(table):
            total = None
            for col in range(knots):
                coef = jnp.zeros(here.shape, F32)
                for g in range(grades):
                    coef = jnp.where(chosen[g], table[g, col], coef)
                total = total + coef * ramps[col - 1] if col else coef
            return total

        remanence = value(rem)
        coercivity = value(coer)
        square = coercivity * coercivity
        res[r] = remanence * square / (square + ready[1, r]) - ready[2, r]
        return 0

    lax.fori_loop(0, rows, body, 0, unroll=16)
    up, down = [
        packed(lambda r, s: roll(res[r], s, 1), rows, width, col) for col in (width - 2, 0)
    ]
    pack_a[...], pack_b[...] = by_parity(is_even(SECTOR), up, down)


def gram_kernel(
    res, own_a, own_b, got_a, got_b, ax_a, ax_b, nu, main, packs, main_side,
    q, kq, sums, x_tall, p_tall, q_tall, s_tall, blurred
):
    rows, depth, width = res.shape
    before, after = inner(AXIAL)
    x_packs = tall_packs(residual_packs(own_a, own_b, got_a, got_b), rows, ax_a, ax_b)
    n_packs = [packs[i] for i in range(4)]
    p_packs = [x * n for x, n in zip(x_packs, n_packs)]
    x_side, n_side, p_side = [side_of(p[0], p[1]) for p in (x_packs, n_packs, p_packs)]
    for i, side in enumerate((x_side, p_side)):
        blurred[i] = radial_blur_side(axial_blur(side))
    q_side = main_side[...] * x_side - n_side * blur_side(*x_packs) - blur_side(*p_packs)
    clear_ends(x_tall, p_tall, q_tall, s_tall)

    def outside(shape):
        place = iota(shape, 0)
        high = jnp.logical_and(place >= depth, place < 2 * depth - 4)
        low = place >= 2 * depth - 4
        return jnp.logical_or(
            jnp.logical_and(low, jnp.logical_not(before)),
            jnp.logical_and(high, jnp.logical_not(after)),
        )

    q_side = jnp.where(outside(q_side.shape), 0.0, q_side)
    for i, side in enumerate((q_side, q_side * n_side)):
        blurred[2 + i] = radial_blur_side(axial_blur(side))

    def fill(r, _):
        x = tall(res[r], *beyond(ax_a, ax_b, r))
        x_tall[r + 1] = x
        p_tall[r + 1] = x * nu[r + 1]
        return 0

    lax.fori_loop(0, rows, fill, 0, unroll=16)
    off = outside((2 * depth, width))

    def image(r, t, shift, carry):
        a, b, c = carry
        near, weighed = [
            around_blur(
                axial_blur(radial_blur(ref, r)),
                pltpu.roll(tile(blurred.at[i], t, 2 * depth), shift, 1),
            )
            for i, ref in ((0, x_tall), (1, p_tall))
        ]
        n = nu[r + 1]
        y = jnp.where(off, 0.0, main[r] * x_tall[r + 1] - n * near - weighed)
        q_tall[r + 1] = y
        s_tall[r + 1] = y * n
        y = y[0:depth]
        q[r] = y
        x = res[r]
        return a + x * x, b + x * y, c + y * y

    none = jnp.zeros((depth, width), F32)
    a, b, c = by_half(rows, width, image, (none, none, none), 32)

    def again(r, t, shift, d):
        near, weighed = [
            around_blur(
                axial_blur(radial_blur(ref, r))[0:depth],
                pltpu.roll(tile(blurred.at[i], t, depth), shift, 1),
            )
            for i, ref in ((2, q_tall), (3, s_tall))
        ]
        x = q[r]
        y = main[r, 0:depth] * x - nu[r + 1, 0:depth] * near - weighed
        kq[r] = y
        return d + y * x

    d = by_half(rows, width, again, none, 32)
    spot = iota((1, width), 1)
    line = jnp.zeros((1, width), F32)
    for i, part in enumerate((a, b, c, d)):
        line = jnp.where(spot == i, jnp.sum(part), line)
    sums[...] = line


def final_kernel(parts, v, res, q, kq, potential, misfit):
    rows = v.shape[0]
    total = parts[...].reshape(parts.shape[0] // 8, 8, parts.shape[1])
    total = jnp.sum(jnp.sum(total, axis=0), axis=0, keepdims=True)
    rr, rq, qq, qk = [total[0:1, i : i + 1] for i in range(4)]
    alpha = rr / rq
    fresh = alpha * alpha * qq - 2.0 * alpha * rq + rr
    ratio = 1.0 + fresh / rr
    bend = ratio * ratio * rq - 2.0 * alpha * ratio * qq + alpha * alpha * qk
    again = fresh / bend
    straight = alpha + again * ratio
    cross = again * alpha
    straight = jnp.broadcast_to(straight, v.shape[1:])
    cross = jnp.broadcast_to(cross, v.shape[1:])

    def body(r, _):
        x, y = res[r], q[r]
        potential[r] = v[r] + (straight * x - cross * y)
        misfit[r] = x - straight * y + cross * kq[r]
        return 0

    lax.fori_loop(0, rows, body, 0, unroll=16)


def local(
    prior_thermal_state,
    stepped_thermal_conductance,
    dissipated_power_input,
    substance_label,
    magnet_quality_line,
    permanent_pole_mask,
    operator_main_entry,
    vector_potential_now,
    reverse_magnetizing_burden,
    inverse_permeability,
    remanence_knot_chart,
    coercivity_knot_chart,
):
    u, k, heat = prior_thermal_state, stepped_thermal_conductance, dissipated_power_input
    v, diag = vector_potential_now, operator_main_entry
    thick, depth, around = u.shape
    rows, _, width = v.shape
    block = (rows, depth, width)
    high = (rows, 2 * depth, width)
    padded = (rows + 2, 2 * depth, width)
    pack = (depth, 2 * rows)
    tall_pack = (2 * depth, 2 * rows)
    per_pack = 2 * rows // width
    sectors = lax.axis_size("chip") * lax.axis_size("core")
    slabs = lax.axis_size(AXIAL)

    row_pair, edge_pair = (2, depth, around), (2 * thick, around)
    *row, edge_a, edge_b = call(
        thermal_edges_kernel,
        [row_pair, row_pair, edge_pair, edge_pair],
        [u, k],
    )
    nu, *own = call(
        prep_kernel,
        [block, (2, *pack), (2, *pack)],
        [v, substance_label, diag, inverse_permeability],
        smem=(3,),
    )
    edge = (thick, around)
    line = (1, depth, around)
    longer = (1, depth, around + 4 * rows)
    faces = (thick + 1, depth, around)
    got = thermal_swaps(*row, edge_a, edge_b)
    u, edge_b, *planes = call(
        first_sweep_kernel,
        [u.shape, edge, faces, u.shape, u.shape, u.shape],
        [u, k, *got, heat],
    )
    *row, edge_a = call(rest_kernel, [longer, longer, edge], [u, *own])
    got = thermal_swaps(*row, edge_a, edge_b)
    static = [*own, *got[:2]]
    spread = (2 * rows + 6 * per_pack, 2, width)
    ax = call(edges_kernel, [spread, spread], [nu, v, diag, *static])
    for _ in range(SWEEPS - 2):
        u, edge_b = call(sweep_kernel, [u.shape, edge], [u, *got, heat, *planes])
        *row, edge_a = call(rest_kernel, [line, line, edge], [u])
        got = thermal_swaps(*row, edge_a, edge_b)
    ax = swapped(*ax, AXIAL)
    (cut,) = call(
        last_sweep_kernel, [(sectors, thick, depth, width)], [u, *got, heat, *planes]
    )
    sector_field = lax.all_to_all(cut, SECTOR, 0, 0).reshape(block)
    (relaxed,) = call(whole_kernel, [u.shape], [cut])
    nu_tall, main, ready, nu_packs, main_side = call(
        setup_kernel,
        [padded, high, (3, *block), (4, *tall_pack), tall_pack],
        [
            v,
            nu,
            diag,
            magnet_quality_line,
            permanent_pole_mask,
            reverse_magnetizing_burden,
            *static,
            *ax,
        ],
        scratch=[
            pltpu.VMEM(padded, F32),
            pltpu.VMEM(padded, F32),
            pltpu.VMEM((3, *tall_pack), F32),
        ],
    )
    res, *own = call(
        residual_kernel,
        [block, pack, pack],
        [sector_field, ready, remanence_knot_chart, coercivity_knot_chart],
        smem=(2, 3),
    )
    packs = [*own, *swapped(*own, SECTOR)]
    spread = (rows + 4 * per_pack, 2, width)
    ax = call(residual_edges_kernel, [spread, spread], [res, *packs])
    q, kq, sums = call(
        gram_kernel,
        [block, block, (1, width)],
        [res, *packs, *swapped(*ax, AXIAL), nu_tall, main, nu_packs, main_side],
        scratch=[pltpu.VMEM(padded, F32)] * 4 + [pltpu.VMEM((4, *tall_pack), F32)],
    )
    sums = sums + lax.ppermute(sums, "core", [(0, 1), (1, 0)])
    chips = sectors * slabs // 2
    sums = jnp.broadcast_to(sums[None], (chips, 1, width))
    sums = lax.all_to_all(sums, ("chip", AXIAL), 0, 0)
    potential, misfit = call(final_kernel, [block, block], [sums.reshape(chips, width), v, res, q, kq])
    return relaxed, potential, misfit


def solution(mesh):
    thermal = P(SECTOR, AXIAL, None)
    magnetic = P(None, AXIAL, SECTOR)
    sectors, slabs = mesh.devices.shape
    cores = mesh.devices.reshape(sectors // 2, 2, slabs)
    return jax.shard_map(
        local,
        mesh=jax.sharding.Mesh(cores, (*SECTOR, AXIAL)),
        in_specs=(thermal,) * 3 + (magnetic,) * 6 + (P(),) * 3,
        out_specs=(thermal, magnetic, magnetic),
        check_vma=False,
    )
```

```python
import jax
import jax.numpy as jnp
from jax import lax
from jax.experimental import pallas as pl
from jax.experimental.pallas import tpu as pltpu
from jax.sharding import PartitionSpec as P

SWEEPS = 4
TABLE = (4, 4)
SECTOR = ("chip", "core")
AXIAL = "axial"
F32 = jnp.float32
MIB = 1024 * 1024


def call(kernel, out_shapes, args, smem=(), scratch=(), vmem=14, micros=1):
    specs = [
        pl.BlockSpec(memory_space=pltpu.SMEM if i in smem else pltpu.VMEM)
        for i in range(len(args))
    ]
    moved = sum(a.size * 4 for a in args)
    return pl.pallas_call(
        kernel,
        out_shape=[jax.ShapeDtypeStruct(s, F32) for s in out_shapes],
        in_specs=specs,
        out_specs=[pl.BlockSpec(memory_space=pltpu.VMEM)] * len(out_shapes),
        scratch_shapes=list(scratch),
        compiler_params=pltpu.CompilerParams(vmem_limit_bytes=vmem * MIB),
        cost_estimate=pl.CostEstimate(
            flops=micros * 1_150_000_000, bytes_accessed=moved, transcendentals=0
        ),
    )(*args)


def roll(x, shift, axis):
    return pltpu.roll(x, shift % x.shape[axis], axis)


def iota(shape, axis):
    return lax.broadcasted_iota(jnp.int32, shape, axis)


def place_on(axis):
    if isinstance(axis, str):
        return lax.axis_index(axis), lax.axis_size(axis)
    major, minor = axis
    size = lax.axis_size(minor)
    return lax.axis_index(major) * size + lax.axis_index(minor), lax.axis_size(major) * size


def is_even(axis):
    return place_on(axis)[0] % 2 == 0


def by_parity(even, a, b):
    return jnp.where(even, a, b), jnp.where(even, b, a)


def swapped(a, b, axis):
    if axis == SECTOR:
        n = lax.axis_size("chip") * lax.axis_size("core")
        first = [(i, i ^ 1) for i in range(n)]
        second = [(i, (i + 1) % n if i % 2 else (i - 1) % n) for i in range(n)]
        return lax.ppermute(a, SECTOR, first), lax.ppermute(b, SECTOR, second)
    n = lax.axis_size(AXIAL)
    first = [(i, i ^ 1) for i in range(n)]
    second = []
    for s in range(lax.axis_size("chip") * lax.axis_size("core")):
        for i in range(n):
            if 0 < i < n - 1:
                second.append((s * n + i, s * n + (i + 1 if i % 2 else i - 1)))
            else:
                second.append((s * n + i, (s ^ 1) * n + i))
    b = lax.ppermute(b, (*SECTOR, AXIAL), second)
    return lax.ppermute(a, AXIAL, first), b


def thermal_swaps(row_a, row_b, edge_a, edge_b):
    edges = swapped(edge_a, edge_b, AXIAL)
    return [*swapped(row_a, row_b, SECTOR), *edges]


def inner(axis):
    place, size = place_on(axis)
    return place > 0, place < size - 1


def thermal_edges_kernel(u, k, edge_a, edge_b):
    rows, depth, _ = u.shape
    even_slab = is_even(AXIAL)
    for i, x in enumerate((u, k)):
        for r in range(rows):
            at = slice(i * rows + r, i * rows + r + 1)
            edge_a[at], edge_b[at] = by_parity(even_slab, x[r, depth - 1 : depth], x[r, 0:1])


def own_fluxes(u, heat, around, radial, minus, plus):
    for r in range(u.shape[0]):
        own = u[r]
        flow = around[r] * (roll(own, -1, 1) - own)
        new = own + (flow - roll(flow, 1, 1)) + 0.16 * heat[r]
        if r > 0:
            new = new + radial[r - 1] * (u[r - 1] - own)
        if r < u.shape[0] - 1:
            new = new + radial[r] * (u[r + 1] - own)
        yield r, new + (
            minus[r] * (roll(own, 1, 0) - own) + plus[r] * (roll(own, -1, 0) - own)
        )


def first_inner_kernel(u, k, heat, part, around, radial, minus, plus):
    rows, depth, _ = u.shape
    for r in range(rows):
        own = k[r]
        place = iota(own.shape, 0)
        around[r] = 0.08 * (own + roll(own, -1, 1))
        minus[r] = jnp.where(place == 0, 0.0, 0.08 * (own + roll(own, 1, 0)))
        plus[r] = jnp.where(place == depth - 1, 0.0, 0.08 * (own + roll(own, -1, 0)))
        if r:
            radial[r - 1] = 0.08 * (own + k[r - 1])
    for r, new in own_fluxes(u, heat, around, radial, minus, plus):
        part[r] = new


def inner_kernel(u, heat, around, radial, minus, plus, part, edge_a):
    even_slab = is_even(AXIAL)
    depth = u.shape[1]
    for r, new in own_fluxes(u, heat, around, radial, minus, plus):
        part[r] = new
        edge_a[r : r + 1] = by_parity(even_slab, u[r, depth - 1 : depth], u[r, 0:1])[0]


def at_ends(low, high, between):
    place = iota(between.shape, 0)
    depth = between.shape[0]
    return jnp.where(place == 0, low, jnp.where(place == depth - 1, high, between))


def edges_of(refs, which, rows, width):
    row_a, row_b, edge_a, edge_b = refs
    above, below = inner(SECTOR)
    before, after = inner(AXIAL)
    even_slab = is_even(AXIAL)
    down, up = by_parity(is_even(SECTOR), row_a[which, :, 0:width], row_b[which, :, 0:width])
    lows, highs = [], []
    for i in range(which * rows, which * rows + rows):
        high, low = by_parity(even_slab, edge_a[i : i + 1], edge_b[i : i + 1])
        lows.append(jnp.where(before, low, 0.0))
        highs.append(jnp.where(after, high, 0.0))
    return jnp.where(above, up, 0.0), jnp.where(below, down, 0.0), lows, highs


def whole_sweep(u, part, edges, ends, rim):
    u_up, u_down, u_low, u_high = edges
    rows = u.shape[0]
    for r in range(rows):
        own = u[r]
        new = part[r] + rim[r] * (at_ends(u_low[r], u_high[r], own) - own)
        if r == 0:
            new = new + ends[0] * (u_up - own)
        if r == rows - 1:
            new = new + ends[1] * (u_down - own)
        yield r, new


def keep_edge(swept, out, edge_b):
    even_slab = is_even(AXIAL)
    for r, new in swept:
        depth = new.shape[0]
        out[r] = new
        edge_b[r : r + 1] = by_parity(even_slab, new[depth - 1 : depth], new[0:1])[1]


def rows_kernel(u, *refs):
    *packs, row_b, row_a = refs
    rows, _, width = u.shape
    row_a[0, :, 0:width], row_b[0, :, 0:width] = by_parity(
        is_even(SECTOR), u[rows - 1], u[0]
    )
    for out, pack in zip((row_a, row_b), packs):
        for i in range(2):
            lanes = pack.shape[2]
            out[0, :, width + i * lanes : width + (i + 1) * lanes] = pack[i]


def first_outer_kernel(
    u, k, part, row_a, row_b, edge_a, edge_b, out, edge_out, ends, rim
):
    refs = (row_a, row_b, edge_a, edge_b)
    rows, _, width = u.shape
    k_up, k_down, k_low, k_high = edges_of(refs, 1, rows, width)
    ends[0] = 0.08 * (k[0] + k_up)
    ends[1] = 0.08 * (k[rows - 1] + k_down)
    for r in range(rows):
        own = k[r]
        rim[r] = at_ends(0.08 * (own + k_low[r]), 0.08 * (own + k_high[r]), 0.0 * own)
    edges = edges_of(refs, 0, rows, width)
    keep_edge(whole_sweep(u, part, edges, ends, rim), out, edge_out)


def outer_kernel(u, part, ends, rim, row_a, row_b, edge_a, edge_b, out, edge_out):
    rows, _, width = u.shape
    edges = edges_of((row_a, row_b, edge_a, edge_b), 0, rows, width)
    keep_edge(whole_sweep(u, part, edges, ends, rim), out, edge_out)


def last_outer_kernel(u, part, ends, rim, row_a, row_b, edge_a, edge_b, *rest):
    cut = rest[-1]
    rows, _, width = u.shape
    edges = edges_of((row_a, row_b, edge_a, edge_b), 0, rows, width)
    for r, new in whole_sweep(u, part, edges, ends, rim):
        for j in range(width // 128):
            cut[j, r] = new[:, 128 * j : 128 * j + 128]


def whole_kernel(cut, out):
    for r in range(out.shape[0]):
        for j in range(cut.shape[0]):
            out[r, :, 128 * j : 128 * j + 128] = cut[j, r]


def packed(tile_of, rows, width, col):
    lane = iota((8, width), 1)
    half = width // 2
    out = []
    for t in range(rows // half):
        acc = jnp.zeros((8, width), F32)
        for i in range(half):
            acc = jnp.where(lane // 2 == i, tile_of(half * t + i, 2 * i - col), acc)
        out.append(acc)
    return jnp.concatenate(out, axis=1)


def nu_kernel(v, label, table, nu):
    rows = v.shape[0]

    def body(r, _):
        kind = label[r]
        base = jnp.full(kind.shape, table[0], F32)
        for m in range(1, table.shape[0]):
            base = jnp.where(kind == m, table[m], base)
        here = v[r]
        nu[r] = base * (1.0 + 0.25 * here * here)
        return 0

    lax.fori_loop(0, rows, body, 0, unroll=16)


def packs_kernel(nu, v, diag, pack_a, pack_b):
    rows, _, width = v.shape
    even = iota((8, width), 1) % 2 == 0
    made = []
    for nu_col, col in ((width - 2, width - 1), (0, 0)):
        pairs = packed(lambda r, s: roll(nu[r], s, 1), rows, width, nu_col)
        mixed = packed(
            lambda r, s: jnp.where(even, roll(v[r], s, 1), roll(diag[r], s + 1, 1)),
            rows,
            width,
            col,
        )
        made.append((pairs, mixed))
    for i in range(2):
        pack_a[i], pack_b[i] = by_parity(is_even(SECTOR), made[0][i], made[1][i])


def put_packs(packs, at, even, out_a, out_b):
    for pack in packs:
        depth, lanes = pack.shape
        for j in range(lanes // 128):
            cut = pack[:, 128 * j : 128 * j + 128]
            out_a[at], out_b[at] = by_parity(even, cut[depth - 2 : depth], cut[0:2])
            at += 1


def put_edges(field, at, even, out_a, out_b):
    rows, depth, _ = field.shape
    out_a[at : at + rows], out_b[at : at + rows] = by_parity(
        even, field[:, depth - 2 : depth, :], field[:, 0:2, :]
    )


def static_packs(own_a, own_b, row_a, row_b):
    even = is_even(SECTOR)
    lanes = own_a.shape[2]
    width = row_a.shape[2] - 2 * lanes
    own_up, own_down = by_parity(even, own_a[0], own_b[0])
    spans = [slice(width + i * lanes, width + (i + 1) * lanes) for i in range(2)]
    nu_high, nu_low = by_parity(even, row_a[0, :, spans[0]], row_b[0, :, spans[0]])
    mix_high, mix_low = by_parity(even, row_a[0, :, spans[1]], row_b[0, :, spans[1]])
    return [nu_low, nu_high, own_down, own_up, mix_low, mix_high]


def edges_kernel(nu, v, diag, own_a, own_b, row_a, row_b, out_b, out_a):
    rows, depth, _ = nu.shape
    even = is_even(AXIAL)
    put_edges(nu, 0, even, out_a, out_b)
    for i, field in enumerate((v, diag)):
        out_a[rows : 2 * rows, i : i + 1], out_b[rows : 2 * rows, i : i + 1] = by_parity(
            even, field[:, depth - 1 : depth, :], field[:, 0:1, :]
        )
    put_packs(static_packs(own_a, own_b, row_a, row_b), 2 * rows, even, out_a, out_b)


def residual_packs(own_a, own_b, got_a, got_b):
    even = is_even(SECTOR)
    up, down = by_parity(even, own_a[...], own_b[...])
    high, low = by_parity(even, got_a[...], got_b[...])
    return [low, high, down, up]


def residual_edges_kernel(res, own_a, own_b, got_a, got_b, out_a, out_b):
    even = is_even(AXIAL)
    put_edges(res, 0, even, out_a, out_b)
    put_packs(residual_packs(own_a, own_b, got_a, got_b), res.shape[0], even, out_a, out_b)


def tall(own, high, low):
    empty = jnp.zeros((own.shape[0] - 4, own.shape[1]), F32)
    return jnp.concatenate([own, high, empty, low], axis=0)


def beyond(ax_a, ax_b, at):
    before, after = inner(AXIAL)
    high, low = by_parity(is_even(AXIAL), ax_a[at], ax_b[at])
    return jnp.where(after, high, 0.0), jnp.where(before, low, 0.0)


def tall_packs(packs, at, ax_a, ax_b):
    out = []
    for pack in packs:
        span = range(at, at + pack.shape[1] // 128)
        pairs = [beyond(ax_a, ax_b, j) for j in span]
        high, low = [jnp.concatenate(parts, axis=1) for parts in zip(*pairs)]
        out.append(tall(pack, high, low))
        at = span.stop
    return out


def side_of(low, high):
    return jnp.where(iota(low.shape, 1) % 2 == 1, low, high)


def axial_blur(x):
    return x + 0.5 * (roll(x, 1, 0) + roll(x, -1, 0))


def radial_blur_side(x):
    lane = iota(x.shape, 1)
    lanes = x.shape[1]
    above = jnp.where(lane < 2, 0.0, roll(x, 2, 1))
    below = jnp.where(lane >= lanes - 2, 0.0, roll(x, -2, 1))
    return x + 0.5 * (above + below)


def blur_side(low, high, down, up):
    left = low + 0.5 * roll(low + down, 1, 1)
    right = high + 0.5 * roll(high + up, -1, 1)
    return radial_blur_side(axial_blur(side_of(left, right)))


def around_blur(x, side):
    lane = iota(x.shape, 1)
    width = x.shape[1]
    before = jnp.where(lane == 0, side, roll(x, 1, 1))
    after = jnp.where(lane == width - 1, side, roll(x, -1, 1))
    return x + 0.5 * (before + after)


def radial_blur(ref, r):
    return ref[r + 1] + 0.5 * (ref[r] + ref[r + 2])


def clear_ends(*refs):
    for ref in refs:
        zero = jnp.zeros(ref.shape[1:], F32)
        ref[0] = zero
        ref[ref.shape[0] - 1] = zero


def by_half(rows, width, body, carry, unroll):
    half = width // 2
    for t in range(rows // half):

        def step(i, c, t=t):
            return body(half * t + i, t, (2 * width - 1 - 2 * i) % width, c)

        carry = lax.fori_loop(0, half, step, carry, unroll=unroll)
    return carry


def tile(ref, t, depth):
    return ref[0:depth, 128 * t : 128 * t + 128]


def ready_kernel(
    v, nu, diag, grade, mask, burden, rem, coer, own_a, own_b, row_a, row_b, ax_a, ax_b,
    ready, nu_tall, v_tall, p_tall, blurred
):
    rows, depth, width = v.shape
    nu_low, nu_high, _, _, mix_low, mix_high = tall_packs(
        static_packs(own_a, own_b, row_a, row_b), 2 * rows, ax_a, ax_b
    )
    odd = iota(mix_low.shape, 1) % 2 == 1
    v_side = jnp.where(odd, roll(mix_low, 1, 1), mix_high)
    nu_side = side_of(nu_low, nu_high)
    for i, side in enumerate((nu_side, v_side, v_side * nu_side)):
        blurred[i] = radial_blur_side(axial_blur(side))
    clear_ends(nu_tall, v_tall, p_tall)
    grades, knots = TABLE
    for i, table in enumerate((rem, coer)):
        for g in range(grades):
            for col in range(knots):
                at = (i * grades + g) * knots + col
                line = jnp.full((1, width), table[g, col], F32)
                ready[3 * rows + at // depth, at % depth : at % depth + 1] = line

    def fill(r, _):
        mixed_high, mixed_low = beyond(ax_a, ax_b, rows + r)
        n = tall(nu[r], *beyond(ax_a, ax_b, r))
        empty = jnp.zeros((depth - 2, width), F32)
        x = jnp.concatenate([v[r], mixed_high[0:1], empty, mixed_low[0:1]], axis=0)
        nu_tall[r + 1] = n
        v_tall[r + 1] = x
        p_tall[r + 1] = x * n
        ready[r] = jnp.where(mask[r] == 1, grade[r], -1).astype(F32)
        ready[rows + r] = burden[r]
        return 0

    lax.fori_loop(0, rows, fill, 0, unroll=16)

    def body(r, t, shift, _):
        field, near, weighed = [
            around_blur(
                axial_blur(radial_blur(ref, r))[0:depth],
                pltpu.roll(tile(blurred.at[i], t, depth), shift, 1),
            )
            for i, ref in enumerate((nu_tall, v_tall, p_tall))
        ]
        n = nu[r]
        ready[2 * rows + r] = (diag[r] + 8.0 * n + field) * v[r] - n * near - weighed
        return 0

    by_half(rows, width, body, 0, 32)


def operator_kernel(
    nu, diag, own_a, own_b, row_a, row_b, ax_a, ax_b, res_a, res_b,
    nu_tall, main, packs, main_side, blurred
):
    rows, depth, width = nu.shape
    nu_low, nu_high, nu_down, nu_up, mix_low, mix_high = tall_packs(
        static_packs(own_a, own_b, row_a, row_b), 2 * rows, ax_a, ax_b
    )
    odd = iota(mix_low.shape, 1) % 2 == 1
    diag_side = jnp.where(odd, mix_low, roll(mix_high, -1, 1))
    nu_side = side_of(nu_low, nu_high)
    for i, pack in enumerate((nu_low, nu_high, nu_down, nu_up)):
        packs[i] = pack
    main_side[...] = diag_side + 8.0 * nu_side + blur_side(nu_low, nu_high, nu_down, nu_up)
    blurred[...] = radial_blur_side(axial_blur(nu_side))
    clear_ends(nu_tall)

    def fill(r, _):
        nu_tall[r + 1] = tall(nu[r], *beyond(ax_a, ax_b, r))
        return 0

    lax.fori_loop(0, rows, fill, 0, unroll=16)

    def body(r, t, shift, _):
        high, low = beyond(ax_a, ax_b, rows + r)
        empty = jnp.zeros((depth - 2, width), F32)
        side = pltpu.roll(tile(blurred, t, 2 * depth), shift, 1)
        field = around_blur(axial_blur(radial_blur(nu_tall, r)), side)
        diag_tall = jnp.concatenate([diag[r], high[1:2], empty, low[1:2]], axis=0)
        main[r] = diag_tall + 8.0 * nu_tall[r + 1] + field
        return 0

    by_half(rows, width, body, 0, 32)


def residual_kernel(t, ready, res, pack_a, pack_b):
    rows, depth, width = t.shape
    grades, knots = TABLE

    def entry(i):
        spot = 3 * rows + i // depth, slice(i % depth, i % depth + 1)
        return jnp.broadcast_to(ready[spot], (depth, width))

    tables = [
        [[entry((i * grades + g) * knots + col) for col in range(knots)] for g in range(grades)]
        for i in range(2)
    ]

    def body(r, _):
        which = ready[r]
        here = t[r]
        chosen = [which == g for g in range(grades)]
        ramps = [jnp.maximum(here - (col - knots // 2), 0.0) for col in range(1, knots)]

        def value(table):
            total = None
            for col in range(knots):
                coef = jnp.zeros(here.shape, F32)
                for g in range(grades):
                    coef = jnp.where(chosen[g], table[g][col], coef)
                total = total + coef * ramps[col - 1] if col else coef
            return total

        remanence, coercivity = [value(table) for table in tables]
        square = coercivity * coercivity
        source = remanence * square / (square + ready[rows + r])
        res[r] = source - ready[2 * rows + r]
        return 0

    lax.fori_loop(0, rows, body, 0, unroll=16)
    up, down = [
        packed(lambda r, s: roll(res[r], s, 1), rows, width, col) for col in (width - 2, 0)
    ]
    pack_a[...], pack_b[...] = by_parity(is_even(SECTOR), up, down)


def gram_kernel(
    res, own_a, own_b, got_a, got_b, ax_a, ax_b, nu, main, packs, main_side,
    q, kq, sums, x_tall, p_tall, q_tall, s_tall, blurred
):
    rows, depth, width = res.shape
    before, after = inner(AXIAL)
    x_packs = tall_packs(residual_packs(own_a, own_b, got_a, got_b), rows, ax_a, ax_b)
    n_packs = [packs[i] for i in range(4)]
    p_packs = [x * n for x, n in zip(x_packs, n_packs)]
    x_side, n_side, p_side = [side_of(p[0], p[1]) for p in (x_packs, n_packs, p_packs)]
    for i, side in enumerate((x_side, p_side)):
        blurred[i] = radial_blur_side(axial_blur(side))
    q_side = main_side[...] * x_side - n_side * blur_side(*x_packs) - blur_side(*p_packs)
    clear_ends(x_tall, p_tall, q_tall, s_tall)

    def outside(shape):
        place = iota(shape, 0)
        high = jnp.logical_and(place >= depth, place < 2 * depth - 4)
        low = place >= 2 * depth - 4
        return jnp.logical_or(
            jnp.logical_and(low, jnp.logical_not(before)),
            jnp.logical_and(high, jnp.logical_not(after)),
        )

    q_side = jnp.where(outside(q_side.shape), 0.0, q_side)
    for i, side in enumerate((q_side, q_side * n_side)):
        blurred[2 + i] = radial_blur_side(axial_blur(side))

    def fill(r, _):
        x = tall(res[r], *beyond(ax_a, ax_b, r))
        x_tall[r + 1] = x
        p_tall[r + 1] = x * nu[r + 1]
        return 0

    lax.fori_loop(0, rows, fill, 0, unroll=16)
    off = outside((2 * depth, width))

    def image(r, t, shift, carry):
        a, b, c = carry
        near, weighed = [
            around_blur(
                axial_blur(radial_blur(ref, r)),
                pltpu.roll(tile(blurred.at[i], t, 2 * depth), shift, 1),
            )
            for i, ref in ((0, x_tall), (1, p_tall))
        ]
        n = nu[r + 1]
        y = jnp.where(off, 0.0, main[r] * x_tall[r + 1] - n * near - weighed)
        q_tall[r + 1] = y
        s_tall[r + 1] = y * n
        y = y[0:depth]
        q[r] = y
        x = res[r]
        return a + x * x, b + x * y, c + y * y

    none = jnp.zeros((depth, width), F32)
    a, b, c = by_half(rows, width, image, (none, none, none), 64)

    def again(r, t, shift, d):
        near, weighed = [
            around_blur(
                axial_blur(radial_blur(ref, r))[0:depth],
                pltpu.roll(tile(blurred.at[i], t, depth), shift, 1),
            )
            for i, ref in ((2, q_tall), (3, s_tall))
        ]
        x = q[r]
        y = main[r, 0:depth] * x - nu[r + 1, 0:depth] * near - weighed
        kq[r] = y
        return d + y * x

    d = by_half(rows, width, again, none, 64)
    spot = iota((1, width), 1)
    line = jnp.zeros((1, width), F32)
    for i, part in enumerate((a, b, c, d)):
        line = jnp.where(spot == i, jnp.sum(part), line)
    sums[...] = line


def final_kernel(parts, v, res, q, kq, potential, misfit):
    rows = v.shape[0]
    total = parts[...].reshape(parts.shape[0] // 8, 8, parts.shape[1])
    total = jnp.sum(jnp.sum(total, axis=0), axis=0, keepdims=True)
    rr, rq, qq, qk = [total[0:1, i : i + 1] for i in range(4)]
    alpha = rr / rq
    fresh = alpha * alpha * qq - 2.0 * alpha * rq + rr
    ratio = 1.0 + fresh / rr
    bend = ratio * ratio * rq - 2.0 * alpha * ratio * qq + alpha * alpha * qk
    again = fresh / bend
    straight = alpha + again * ratio
    cross = again * alpha
    straight = jnp.broadcast_to(straight, v.shape[1:])
    cross = jnp.broadcast_to(cross, v.shape[1:])

    def body(r, _):
        x, y = res[r], q[r]
        potential[r] = v[r] + (straight * x - cross * y)
        misfit[r] = x - straight * y + cross * kq[r]
        return 0

    lax.fori_loop(0, rows, body, 0, unroll=16)


def local(
    prior_thermal_state,
    stepped_thermal_conductance,
    dissipated_power_input,
    substance_label,
    magnet_quality_line,
    permanent_pole_mask,
    operator_main_entry,
    vector_potential_now,
    reverse_magnetizing_burden,
    inverse_permeability,
    remanence_knot_chart,
    coercivity_knot_chart,
):
    u, k, heat = prior_thermal_state, stepped_thermal_conductance, dissipated_power_input
    v, diag = vector_potential_now, operator_main_entry
    thick, depth, around = u.shape
    rows, _, width = v.shape
    block = (rows, depth, width)
    high = (rows, 2 * depth, width)
    padded = (rows + 2, 2 * depth, width)
    pack = (depth, 2 * rows)
    tall_pack = (2 * depth, 2 * rows)
    per_pack = 2 * rows // width
    sectors = lax.axis_size("chip") * lax.axis_size("core")
    slabs = lax.axis_size(AXIAL)

    last, first = by_parity(is_even(SECTOR), thick - 1, 0)
    row = [
        jnp.concatenate([lax.dynamic_slice_in_dim(x, at, 1) for x in (u, k)])
        for at in (last, first)
    ]
    edge_pair = (2 * thick, around)
    edge_a, edge_b = call(thermal_edges_kernel, [edge_pair, edge_pair], [u, k])
    (nu,) = call(nu_kernel, [block], [v, substance_label, inverse_permeability], smem=(2,))
    own = call(packs_kernel, [(2, *pack), (2, *pack)], [nu, v, diag], micros=2)
    edge = (thick, around)
    line = (1, depth, around)
    longer = (1, depth, around + 4 * rows)
    inner_faces = (thick - 1, depth, around)
    part, *planes = call(
        first_inner_kernel,
        [u.shape, u.shape, inner_faces, u.shape, u.shape],
        [u, k, heat],
        micros=2,
    )
    got = thermal_swaps(*row, edge_a, edge_b)
    u, edge_b, *faces = call(
        first_outer_kernel,
        [u.shape, edge, (2, depth, around), u.shape],
        [u, k, part, *got],
    )
    for step in range(1, SWEEPS):
        more = own if step == 2 else []
        one = longer if step == 2 else line
        row_b, row_a = call(rows_kernel, [one, one], [u, *more], micros=10)
        part, edge_a = call(inner_kernel, [u.shape, edge], [u, heat, *planes], micros=2)
        got = thermal_swaps(row_a, row_b, edge_a, edge_b)
        if step == 2:
            static = [*own, *got[:2]]
        if step < SWEEPS - 1:
            u, edge_b = call(outer_kernel, [u.shape, edge], [u, part, *faces, *got])
    spread = (2 * rows + 6 * per_pack, 2, width)
    ax = call(edges_kernel, [spread, spread], [nu, v, diag, *static])[::-1]
    (cut,) = call(
        last_outer_kernel, [(sectors, thick, depth, width)], [u, part, *faces, *got]
    )
    ax = swapped(*ax, AXIAL)
    sector_field = lax.all_to_all(cut, SECTOR, 0, 0).reshape(block)
    (relaxed,) = call(whole_kernel, [u.shape], [cut])
    (ready,) = call(
        ready_kernel,
        [(3 * rows + 2 * TABLE[0] * TABLE[1] // depth, depth, width)],
        [
            v,
            nu,
            diag,
            magnet_quality_line,
            permanent_pole_mask,
            reverse_magnetizing_burden,
            remanence_knot_chart,
            coercivity_knot_chart,
            *static,
            *ax,
        ],
        smem=(6, 7),
        micros=3,
        scratch=[pltpu.VMEM(padded, F32)] * 3 + [pltpu.VMEM((3, *tall_pack), F32)],
    )
    res, *own = call(
        residual_kernel,
        [block, pack, pack],
        [sector_field, ready],
        micros=2,
    )
    nu_tall, main, nu_packs, main_side = call(
        operator_kernel,
        [padded, high, (4, *tall_pack), tall_pack],
        [nu, diag, *static, *ax, *own],
        micros=2,
        scratch=[pltpu.VMEM(tall_pack, F32)],
    )
    packs = [*own, *swapped(*own, SECTOR)]
    spread = (rows + 4 * per_pack, 2, width)
    ax = call(residual_edges_kernel, [spread, spread], [res, *packs])
    q, kq, sums = call(
        gram_kernel,
        [block, block, (1, width)],
        [res, *packs, *swapped(*ax, AXIAL), nu_tall, main, nu_packs, main_side],
        scratch=[pltpu.VMEM(padded, F32)] * 4 + [pltpu.VMEM((4, *tall_pack), F32)],
        micros=4,
    )
    sums = sums + lax.ppermute(sums, "core", [(0, 1), (1, 0)])
    chips = sectors * slabs // 2
    sums = jnp.broadcast_to(sums[None], (chips, 1, width))
    sums = lax.all_to_all(sums, ("chip", AXIAL), 0, 0)
    potential, misfit = call(final_kernel, [block, block], [sums.reshape(chips, width), v, res, q, kq])
    return relaxed, potential, misfit


def solution(mesh):
    thermal = P(SECTOR, AXIAL, None)
    magnetic = P(None, AXIAL, SECTOR)
    sectors, slabs = mesh.devices.shape
    cores = mesh.devices.reshape(sectors // 2, 2, slabs)
    return jax.shard_map(
        local,
        mesh=jax.sharding.Mesh(cores, (*SECTOR, AXIAL)),
        in_specs=(thermal,) * 3 + (magnetic,) * 6 + (P(),) * 3,
        out_specs=(thermal, magnetic, magnetic),
        check_vma=False,
    )
```

```python
import jax
import jax.numpy as jnp
from jax import lax
from jax.experimental import pallas as pl
from jax.experimental.pallas import tpu as pltpu
from jax.sharding import PartitionSpec as P

SWEEPS = 4
TABLE = (4, 4)
SECTOR = ("chip", "core")
AXIAL = "axial"
F32 = jnp.float32
MIB = 1024 * 1024


def call(kernel, out_shapes, args, smem=(), scratch=(), vmem=14, micros=1):
    specs = [
        pl.BlockSpec(memory_space=pltpu.SMEM if i in smem else pltpu.VMEM)
        for i in range(len(args))
    ]
    moved = sum(a.size * 4 for a in args)
    return pl.pallas_call(
        kernel,
        out_shape=[jax.ShapeDtypeStruct(s, F32) for s in out_shapes],
        in_specs=specs,
        out_specs=[pl.BlockSpec(memory_space=pltpu.VMEM)] * len(out_shapes),
        scratch_shapes=list(scratch),
        compiler_params=pltpu.CompilerParams(vmem_limit_bytes=vmem * MIB),
        cost_estimate=pl.CostEstimate(
            flops=micros * 1_150_000_000, bytes_accessed=moved if micros else 0, transcendentals=0
        ),
    )(*args)


def roll(x, shift, axis):
    return pltpu.roll(x, shift % x.shape[axis], axis)


def iota(shape, axis):
    return lax.broadcasted_iota(jnp.int32, shape, axis)


def place_on(axis):
    if isinstance(axis, str):
        return lax.axis_index(axis), lax.axis_size(axis)
    major, minor = axis
    size = lax.axis_size(minor)
    return lax.axis_index(major) * size + lax.axis_index(minor), lax.axis_size(major) * size


def is_even(axis):
    return place_on(axis)[0] % 2 == 0


def by_parity(even, a, b):
    return jnp.where(even, a, b), jnp.where(even, b, a)


def swapped(a, b, axis):
    if axis == SECTOR:
        n = lax.axis_size("chip") * lax.axis_size("core")
        first = [(i, i ^ 1) for i in range(n)]
        second = [(i, (i + 1) % n if i % 2 else (i - 1) % n) for i in range(n)]
        return lax.ppermute(a, SECTOR, first), lax.ppermute(b, SECTOR, second)
    n = lax.axis_size(AXIAL)
    first = [(i, i ^ 1) for i in range(n)]
    second = []
    for s in range(lax.axis_size("chip") * lax.axis_size("core")):
        for i in range(n):
            if 0 < i < n - 1:
                second.append((s * n + i, s * n + (i + 1 if i % 2 else i - 1)))
            else:
                second.append((s * n + i, (s ^ 1) * n + i))
    b = lax.ppermute(b, (*SECTOR, AXIAL), second)
    return lax.ppermute(a, AXIAL, first), b


def thermal_swaps(row_a, row_b, edge_a, edge_b):
    edges = swapped(edge_a, edge_b, AXIAL)
    return [*swapped(row_a, row_b, SECTOR), *edges]


def inner(axis):
    place, size = place_on(axis)
    return place > 0, place < size - 1


def thermal_edges_kernel(u, k, edge_a, edge_b):
    rows, depth, _ = u.shape
    even_slab = is_even(AXIAL)
    for i, x in enumerate((u, k)):
        for r in range(rows):
            at = slice(i * rows + r, i * rows + r + 1)
            edge_a[at], edge_b[at] = by_parity(even_slab, x[r, depth - 1 : depth], x[r, 0:1])


def own_fluxes(u, heat, around, radial, minus, plus):
    for r in range(u.shape[0]):
        own = u[r]
        flow = around[r] * (roll(own, -1, 1) - own)
        new = own + (flow - roll(flow, 1, 1)) + 0.16 * heat[r]
        if r > 0:
            new = new + radial[r - 1] * (u[r - 1] - own)
        if r < u.shape[0] - 1:
            new = new + radial[r] * (u[r + 1] - own)
        yield r, new + (
            minus[r] * (roll(own, 1, 0) - own) + plus[r] * (roll(own, -1, 0) - own)
        )


def first_inner_kernel(u, k, heat, part, around, radial, minus, plus):
    rows, depth, _ = u.shape
    for r in range(rows):
        own = k[r]
        place = iota(own.shape, 0)
        around[r] = 0.08 * (own + roll(own, -1, 1))
        minus[r] = jnp.where(place == 0, 0.0, 0.08 * (own + roll(own, 1, 0)))
        plus[r] = jnp.where(place == depth - 1, 0.0, 0.08 * (own + roll(own, -1, 0)))
        if r:
            radial[r - 1] = 0.08 * (own + k[r - 1])
    for r, new in own_fluxes(u, heat, around, radial, minus, plus):
        part[r] = new


def inner_kernel(u, heat, around, radial, minus, plus, part):
    for r, new in own_fluxes(u, heat, around, radial, minus, plus):
        part[r] = new


def at_ends(low, high, between):
    place = iota(between.shape, 0)
    depth = between.shape[0]
    return jnp.where(place == 0, low, jnp.where(place == depth - 1, high, between))


def edges_of(refs, which, rows, width):
    row_a, row_b, edge_a, edge_b = refs
    above, below = inner(SECTOR)
    before, after = inner(AXIAL)
    even_slab = is_even(AXIAL)
    down, up = by_parity(is_even(SECTOR), row_a[which, :, 0:width], row_b[which, :, 0:width])
    lows, highs = [], []
    for i in range(which * rows, which * rows + rows):
        high, low = by_parity(even_slab, edge_a[i : i + 1], edge_b[i : i + 1])
        lows.append(jnp.where(before, low, 0.0))
        highs.append(jnp.where(after, high, 0.0))
    return jnp.where(above, up, 0.0), jnp.where(below, down, 0.0), lows, highs


def whole_sweep(u, part, edges, ends, rim):
    u_up, u_down, u_low, u_high = edges
    rows = u.shape[0]
    for r in range(rows):
        own = u[r]
        new = part[r] + rim[r] * (at_ends(u_low[r], u_high[r], own) - own)
        if r == 0:
            new = new + ends[0] * (u_up - own)
        if r == rows - 1:
            new = new + ends[1] * (u_down - own)
        yield r, new


def ends_kernel(u, edge_b, edge_a):
    depth = u.shape[1]
    even_slab = is_even(AXIAL)
    for r in range(u.shape[0]):
        edge_a[r : r + 1], edge_b[r : r + 1] = by_parity(
            even_slab, u[r, depth - 1 : depth], u[r, 0:1]
        )


def keep_rows(swept, rows, packs, out, row_b, row_a):
    even = is_even(SECTOR)
    for r, new in swept:
        width = new.shape[1]
        out[r] = new
        if r == 0:
            first = new
    row_a[0, :, 0:width], row_b[0, :, 0:width] = by_parity(even, new, first)
    for send, pack in zip((row_a, row_b), packs):
        for i in range(2):
            lanes = pack.shape[2]
            send[0, :, width + i * lanes : width + (i + 1) * lanes] = pack[i]


def first_outer_kernel(
    u, k, part, row_a, row_b, edge_a, edge_b, out, *rest
):
    sent, (ends, rim) = rest[:2], rest[2:]
    refs = (row_a, row_b, edge_a, edge_b)
    rows, _, width = u.shape
    k_up, k_down, k_low, k_high = edges_of(refs, 1, rows, width)
    ends[0] = 0.08 * (k[0] + k_up)
    ends[1] = 0.08 * (k[rows - 1] + k_down)
    for r in range(rows):
        own = k[r]
        rim[r] = at_ends(0.08 * (own + k_low[r]), 0.08 * (own + k_high[r]), 0.0 * own)
    edges = edges_of(refs, 0, rows, width)
    keep_rows(whole_sweep(u, part, edges, ends, rim), rows, [], out, *sent)


def outer_kernel(u, part, ends, rim, row_a, row_b, edge_a, edge_b, *rest):
    packs, kept = rest[:-3], rest[-3:]
    rows, _, width = u.shape
    edges = edges_of((row_a, row_b, edge_a, edge_b), 0, rows, width)
    keep_rows(whole_sweep(u, part, edges, ends, rim), rows, packs, *kept)


def last_outer_kernel(u, part, ends, rim, row_a, row_b, edge_a, edge_b, *rest):
    cut = rest[-1]
    rows, _, width = u.shape
    edges = edges_of((row_a, row_b, edge_a, edge_b), 0, rows, width)
    for r, new in whole_sweep(u, part, edges, ends, rim):
        for j in range(width // 128):
            cut[j, r] = new[:, 128 * j : 128 * j + 128]


def whole_kernel(cut, out):
    for r in range(out.shape[0]):
        for j in range(cut.shape[0]):
            out[r, :, 128 * j : 128 * j + 128] = cut[j, r]


def packed(tile_of, rows, width, col):
    lane = iota((8, width), 1)
    half = width // 2
    out = []
    for t in range(rows // half):
        acc = jnp.zeros((8, width), F32)
        for i in range(half):
            acc = jnp.where(lane // 2 == i, tile_of(half * t + i, 2 * i - col), acc)
        out.append(acc)
    return jnp.concatenate(out, axis=1)


def nu_kernel(v, label, table, nu):
    rows = v.shape[0]

    def body(r, _):
        kind = label[r]
        base = jnp.full(kind.shape, table[0], F32)
        for m in range(1, table.shape[0]):
            base = jnp.where(kind == m, table[m], base)
        here = v[r]
        nu[r] = base * (1.0 + 0.25 * here * here)
        return 0

    lax.fori_loop(0, rows, body, 0, unroll=16)


def packs_kernel(nu, v, diag, pack_a, pack_b):
    rows, _, width = v.shape
    even = iota((8, width), 1) % 2 == 0
    made = []
    for nu_col, col in ((width - 2, width - 1), (0, 0)):
        pairs = packed(lambda r, s: roll(nu[r], s, 1), rows, width, nu_col)
        mixed = packed(
            lambda r, s: jnp.where(even, roll(v[r], s, 1), roll(diag[r], s + 1, 1)),
            rows,
            width,
            col,
        )
        made.append((pairs, mixed))
    for i in range(2):
        pack_a[i], pack_b[i] = by_parity(is_even(SECTOR), made[0][i], made[1][i])


def put_packs(packs, at, even, out_a, out_b):
    for pack in packs:
        depth, lanes = pack.shape
        for j in range(lanes // 128):
            cut = pack[:, 128 * j : 128 * j + 128]
            out_a[at], out_b[at] = by_parity(even, cut[depth - 2 : depth], cut[0:2])
            at += 1


def put_edges(field, at, even, out_a, out_b):
    rows, depth, _ = field.shape
    out_a[at : at + rows], out_b[at : at + rows] = by_parity(
        even, field[:, depth - 2 : depth, :], field[:, 0:2, :]
    )


def static_packs(own_a, own_b, row_a, row_b):
    even = is_even(SECTOR)
    lanes = own_a.shape[2]
    width = row_a.shape[2] - 2 * lanes
    own_up, own_down = by_parity(even, own_a[0], own_b[0])
    spans = [slice(width + i * lanes, width + (i + 1) * lanes) for i in range(2)]
    nu_high, nu_low = by_parity(even, row_a[0, :, spans[0]], row_b[0, :, spans[0]])
    mix_high, mix_low = by_parity(even, row_a[0, :, spans[1]], row_b[0, :, spans[1]])
    return [nu_low, nu_high, own_down, own_up, mix_low, mix_high]


def edges_kernel(nu, v, diag, own_a, own_b, row_a, row_b, out_b, out_a):
    rows, depth, _ = nu.shape
    even = is_even(AXIAL)
    put_edges(nu, 0, even, out_a, out_b)
    for i, field in enumerate((v, diag)):
        out_a[rows : 2 * rows, i : i + 1], out_b[rows : 2 * rows, i : i + 1] = by_parity(
            even, field[:, depth - 1 : depth, :], field[:, 0:1, :]
        )
    put_packs(static_packs(own_a, own_b, row_a, row_b), 2 * rows, even, out_a, out_b)


def residual_packs(own_a, own_b, got_a, got_b):
    even = is_even(SECTOR)
    up, down = by_parity(even, own_a[...], own_b[...])
    high, low = by_parity(even, got_a[...], got_b[...])
    return [low, high, down, up]


def residual_edges_kernel(res, own_a, own_b, got_a, got_b, out_a, out_b):
    even = is_even(AXIAL)
    put_edges(res, 0, even, out_a, out_b)
    put_packs(residual_packs(own_a, own_b, got_a, got_b), res.shape[0], even, out_a, out_b)


def tall(own, high, low):
    empty = jnp.zeros((own.shape[0] - 4, own.shape[1]), F32)
    return jnp.concatenate([own, high, empty, low], axis=0)


def beyond(ax_a, ax_b, at):
    before, after = inner(AXIAL)
    high, low = by_parity(is_even(AXIAL), ax_a[at], ax_b[at])
    return jnp.where(after, high, 0.0), jnp.where(before, low, 0.0)


def tall_packs(packs, at, ax_a, ax_b):
    out = []
    for pack in packs:
        span = range(at, at + pack.shape[1] // 128)
        pairs = [beyond(ax_a, ax_b, j) for j in span]
        high, low = [jnp.concatenate(parts, axis=1) for parts in zip(*pairs)]
        out.append(tall(pack, high, low))
        at = span.stop
    return out


def side_of(low, high):
    return jnp.where(iota(low.shape, 1) % 2 == 1, low, high)


def axial_blur(x):
    return x + 0.5 * (roll(x, 1, 0) + roll(x, -1, 0))


def radial_blur_side(x):
    lane = iota(x.shape, 1)
    lanes = x.shape[1]
    above = jnp.where(lane < 2, 0.0, roll(x, 2, 1))
    below = jnp.where(lane >= lanes - 2, 0.0, roll(x, -2, 1))
    return x + 0.5 * (above + below)


def blur_side(low, high, down, up):
    left = low + 0.5 * roll(low + down, 1, 1)
    right = high + 0.5 * roll(high + up, -1, 1)
    return radial_blur_side(axial_blur(side_of(left, right)))


def around_blur(x, side):
    lane = iota(x.shape, 1)
    width = x.shape[1]
    before = jnp.where(lane == 0, side, roll(x, 1, 1))
    after = jnp.where(lane == width - 1, side, roll(x, -1, 1))
    return x + 0.5 * (before + after)


def radial_blur(ref, r):
    return ref[r + 1] + 0.5 * (ref[r] + ref[r + 2])


def clear_ends(*refs):
    for ref in refs:
        zero = jnp.zeros(ref.shape[1:], F32)
        ref[0] = zero
        ref[ref.shape[0] - 1] = zero


def by_half(rows, width, body, carry, unroll):
    half = width // 2
    for t in range(rows // half):

        def step(i, c, t=t):
            return body(half * t + i, t, (2 * width - 1 - 2 * i) % width, c)

        carry = lax.fori_loop(0, half, step, carry, unroll=unroll)
    return carry


def tile(ref, t, depth):
    return ref[0:depth, 128 * t : 128 * t + 128]


def ready_kernel(
    v, nu, diag, grade, mask, burden, rem, coer, own_a, own_b, row_a, row_b, ax_a, ax_b,
    ready, nu_tall, v_tall, p_tall, blurred
):
    rows, depth, width = v.shape
    nu_low, nu_high, _, _, mix_low, mix_high = tall_packs(
        static_packs(own_a, own_b, row_a, row_b), 2 * rows, ax_a, ax_b
    )
    odd = iota(mix_low.shape, 1) % 2 == 1
    v_side = jnp.where(odd, roll(mix_low, 1, 1), mix_high)
    nu_side = side_of(nu_low, nu_high)
    for i, side in enumerate((nu_side, v_side, v_side * nu_side)):
        blurred[i] = radial_blur_side(axial_blur(side))
    clear_ends(nu_tall, v_tall, p_tall)
    grades, knots = TABLE
    for i, table in enumerate((rem, coer)):
        for g in range(grades):
            for col in range(knots):
                at = (i * grades + g) * knots + col
                line = jnp.full((1, width), table[g, col], F32)
                ready[3 * rows + at // depth, at % depth : at % depth + 1] = line

    def fill(r, _):
        mixed_high, mixed_low = beyond(ax_a, ax_b, rows + r)
        n = tall(nu[r], *beyond(ax_a, ax_b, r))
        empty = jnp.zeros((depth - 2, width), F32)
        x = jnp.concatenate([v[r], mixed_high[0:1], empty, mixed_low[0:1]], axis=0)
        nu_tall[r + 1] = n
        v_tall[r + 1] = x
        p_tall[r + 1] = x * n
        ready[r] = jnp.where(mask[r] == 1, grade[r], -1).astype(F32)
        ready[rows + r] = burden[r]
        return 0

    lax.fori_loop(0, rows, fill, 0, unroll=16)

    def body(r, t, shift, _):
        field, near, weighed = [
            around_blur(
                axial_blur(radial_blur(ref, r))[0:depth],
                pltpu.roll(tile(blurred.at[i], t, depth), shift, 1),
            )
            for i, ref in enumerate((nu_tall, v_tall, p_tall))
        ]
        n = nu[r]
        ready[2 * rows + r] = (diag[r] + 8.0 * n + field) * v[r] - n * near - weighed
        return 0

    by_half(rows, width, body, 0, 32)


def operator_kernel(
    nu, diag, own_a, own_b, row_a, row_b, ax_a, ax_b, res_a, res_b,
    nu_tall, main, packs, main_side, blurred
):
    rows, depth, width = nu.shape
    nu_low, nu_high, nu_down, nu_up, mix_low, mix_high = tall_packs(
        static_packs(own_a, own_b, row_a, row_b), 2 * rows, ax_a, ax_b
    )
    odd = iota(mix_low.shape, 1) % 2 == 1
    diag_side = jnp.where(odd, mix_low, roll(mix_high, -1, 1))
    nu_side = side_of(nu_low, nu_high)
    for i, pack in enumerate((nu_low, nu_high, nu_down, nu_up)):
        packs[i] = pack
    main_side[...] = diag_side + 8.0 * nu_side + blur_side(nu_low, nu_high, nu_down, nu_up)
    blurred[...] = radial_blur_side(axial_blur(nu_side))
    clear_ends(nu_tall)

    def fill(r, _):
        nu_tall[r + 1] = tall(nu[r], *beyond(ax_a, ax_b, r))
        return 0

    lax.fori_loop(0, rows, fill, 0, unroll=16)

    def body(r, t, shift, _):
        high, low = beyond(ax_a, ax_b, rows + r)
        empty = jnp.zeros((depth - 2, width), F32)
        side = pltpu.roll(tile(blurred, t, 2 * depth), shift, 1)
        field = around_blur(axial_blur(radial_blur(nu_tall, r)), side)
        diag_tall = jnp.concatenate([diag[r], high[1:2], empty, low[1:2]], axis=0)
        main[r] = diag_tall + 8.0 * nu_tall[r + 1] + field
        return 0

    by_half(rows, width, body, 0, 32)


def residual_kernel(t, ready, res, pack_a, pack_b):
    rows, depth, width = t.shape
    grades, knots = TABLE

    def entry(i):
        spot = 3 * rows + i // depth, slice(i % depth, i % depth + 1)
        return jnp.broadcast_to(ready[spot], (depth, width))

    tables = [
        [[entry((i * grades + g) * knots + col) for col in range(knots)] for g in range(grades)]
        for i in range(2)
    ]

    def body(r, _):
        which = ready[r]
        here = t[r]
        chosen = [which == g for g in range(grades)]
        ramps = [jnp.maximum(here - (col - knots // 2), 0.0) for col in range(1, knots)]

        def value(table):
            total = None
            for col in range(knots):
                coef = jnp.zeros(here.shape, F32)
                for g in range(grades):
                    coef = jnp.where(chosen[g], table[g][col], coef)
                total = total + coef * ramps[col - 1] if col else coef
            return total

        remanence, coercivity = [value(table) for table in tables]
        square = coercivity * coercivity
        source = remanence * square / (square + ready[rows + r])
        res[r] = source - ready[2 * rows + r]
        return 0

    lax.fori_loop(0, rows, body, 0, unroll=16)
    up, down = [
        packed(lambda r, s: roll(res[r], s, 1), rows, width, col) for col in (width - 2, 0)
    ]
    pack_a[...], pack_b[...] = by_parity(is_even(SECTOR), up, down)


def gram_kernel(
    res, own_a, own_b, got_a, got_b, ax_a, ax_b, nu, main, packs, main_side,
    q, kq, sums, x_tall, p_tall, q_tall, s_tall, blurred
):
    rows, depth, width = res.shape
    before, after = inner(AXIAL)
    x_packs = tall_packs(residual_packs(own_a, own_b, got_a, got_b), rows, ax_a, ax_b)
    n_packs = [packs[i] for i in range(4)]
    p_packs = [x * n for x, n in zip(x_packs, n_packs)]
    x_side, n_side, p_side = [side_of(p[0], p[1]) for p in (x_packs, n_packs, p_packs)]
    for i, side in enumerate((x_side, p_side)):
        blurred[i] = radial_blur_side(axial_blur(side))
    q_side = main_side[...] * x_side - n_side * blur_side(*x_packs) - blur_side(*p_packs)
    clear_ends(x_tall, p_tall, q_tall, s_tall)

    def outside(shape):
        place = iota(shape, 0)
        high = jnp.logical_and(place >= depth, place < 2 * depth - 4)
        low = place >= 2 * depth - 4
        return jnp.logical_or(
            jnp.logical_and(low, jnp.logical_not(before)),
            jnp.logical_and(high, jnp.logical_not(after)),
        )

    q_side = jnp.where(outside(q_side.shape), 0.0, q_side)
    for i, side in enumerate((q_side, q_side * n_side)):
        blurred[2 + i] = radial_blur_side(axial_blur(side))

    def fill(r, _):
        x = tall(res[r], *beyond(ax_a, ax_b, r))
        x_tall[r + 1] = x
        p_tall[r + 1] = x * nu[r + 1]
        return 0

    lax.fori_loop(0, rows, fill, 0, unroll=16)
    off = outside((2 * depth, width))

    def image(r, t, shift, carry):
        a, b, c = carry
        near, weighed = [
            around_blur(
                axial_blur(radial_blur(ref, r)),
                pltpu.roll(tile(blurred.at[i], t, 2 * depth), shift, 1),
            )
            for i, ref in ((0, x_tall), (1, p_tall))
        ]
        n = nu[r + 1]
        y = jnp.where(off, 0.0, main[r] * x_tall[r + 1] - n * near - weighed)
        q_tall[r + 1] = y
        s_tall[r + 1] = y * n
        y = y[0:depth]
        q[r] = y
        x = res[r]
        return a + x * x, b + x * y, c + y * y

    none = jnp.zeros((depth, width), F32)
    a, b, c = by_half(rows, width, image, (none, none, none), 64)

    def again(r, t, shift, d):
        near, weighed = [
            around_blur(
                axial_blur(radial_blur(ref, r))[0:depth],
                pltpu.roll(tile(blurred.at[i], t, depth), shift, 1),
            )
            for i, ref in ((2, q_tall), (3, s_tall))
        ]
        x = q[r]
        y = main[r, 0:depth] * x - nu[r + 1, 0:depth] * near - weighed
        kq[r] = y
        return d + y * x

    d = by_half(rows, width, again, none, 64)
    spot = iota((1, width), 1)
    line = jnp.zeros((1, width), F32)
    for i, part in enumerate((a, b, c, d)):
        line = jnp.where(spot == i, jnp.sum(part), line)
    sums[...] = line


def final_kernel(parts, v, res, q, kq, potential, misfit):
    rows = v.shape[0]
    total = parts[...].reshape(parts.shape[0] // 8, 8, parts.shape[1])
    total = jnp.sum(jnp.sum(total, axis=0), axis=0, keepdims=True)
    rr, rq, qq, qk = [total[0:1, i : i + 1] for i in range(4)]
    alpha = rr / rq
    fresh = alpha * alpha * qq - 2.0 * alpha * rq + rr
    ratio = 1.0 + fresh / rr
    bend = ratio * ratio * rq - 2.0 * alpha * ratio * qq + alpha * alpha * qk
    again = fresh / bend
    straight = alpha + again * ratio
    cross = again * alpha
    straight = jnp.broadcast_to(straight, v.shape[1:])
    cross = jnp.broadcast_to(cross, v.shape[1:])

    def body(r, _):
        x, y = res[r], q[r]
        potential[r] = v[r] + (straight * x - cross * y)
        misfit[r] = x - straight * y + cross * kq[r]
        return 0

    lax.fori_loop(0, rows, body, 0, unroll=16)


def local(
    prior_thermal_state,
    stepped_thermal_conductance,
    dissipated_power_input,
    substance_label,
    magnet_quality_line,
    permanent_pole_mask,
    operator_main_entry,
    vector_potential_now,
    reverse_magnetizing_burden,
    inverse_permeability,
    remanence_knot_chart,
    coercivity_knot_chart,
):
    u, k, heat = prior_thermal_state, stepped_thermal_conductance, dissipated_power_input
    v, diag = vector_potential_now, operator_main_entry
    thick, depth, around = u.shape
    rows, _, width = v.shape
    block = (rows, depth, width)
    high = (rows, 2 * depth, width)
    padded = (rows + 2, 2 * depth, width)
    pack = (depth, 2 * rows)
    tall_pack = (2 * depth, 2 * rows)
    per_pack = 2 * rows // width
    sectors = lax.axis_size("chip") * lax.axis_size("core")
    slabs = lax.axis_size(AXIAL)

    last, first = by_parity(is_even(SECTOR), thick - 1, 0)
    row = [
        jnp.concatenate([lax.dynamic_slice_in_dim(x, at, 1) for x in (u, k)])
        for at in (last, first)
    ]
    edge_pair = (2 * thick, around)
    edge_a, edge_b = call(thermal_edges_kernel, [edge_pair, edge_pair], [u, k])
    (nu,) = call(nu_kernel, [block], [v, substance_label, inverse_permeability], smem=(2,))
    own = call(packs_kernel, [(2, *pack), (2, *pack)], [nu, v, diag], micros=2)
    edge = (thick, around)
    line = (1, depth, around)
    longer = (1, depth, around + 4 * rows)
    inner_faces = (thick - 1, depth, around)
    part, *planes = call(
        first_inner_kernel,
        [u.shape, u.shape, inner_faces, u.shape, u.shape],
        [u, k, heat],
        micros=2,
    )
    got = thermal_swaps(*row, edge_a, edge_b)
    u, row_b, row_a, *faces = call(
        first_outer_kernel,
        [u.shape, line, line, (2, depth, around), u.shape],
        [u, k, part, *got],
    )
    for step in range(1, SWEEPS):
        edge_b, edge_a = call(ends_kernel, [edge, edge], [u], micros=0)
        (part,) = call(inner_kernel, [u.shape], [u, heat, *planes], micros=0)
        got = thermal_swaps(row_a, row_b, edge_a, edge_b)
        if step == 2:
            static = [*own, *got[:2]]
        if step < SWEEPS - 1:
            more = own if step == 1 else []
            one = longer if step == 1 else line
            u, row_b, row_a = call(
                outer_kernel, [u.shape, one, one], [u, part, *faces, *got, *more]
            )
    spread = (2 * rows + 6 * per_pack, 2, width)
    ax = call(edges_kernel, [spread, spread], [nu, v, diag, *static])[::-1]
    (cut,) = call(
        last_outer_kernel, [(sectors, thick, depth, width)], [u, part, *faces, *got]
    )
    ax = swapped(*ax, AXIAL)
    sector_field = lax.all_to_all(cut, SECTOR, 0, 0).reshape(block)
    (relaxed,) = call(whole_kernel, [u.shape], [cut])
    (ready,) = call(
        ready_kernel,
        [(3 * rows + 2 * TABLE[0] * TABLE[1] // depth, depth, width)],
        [
            v,
            nu,
            diag,
            magnet_quality_line,
            permanent_pole_mask,
            reverse_magnetizing_burden,
            remanence_knot_chart,
            coercivity_knot_chart,
            *static,
            *ax,
        ],
        smem=(6, 7),
        micros=3,
        scratch=[pltpu.VMEM(padded, F32)] * 3 + [pltpu.VMEM((3, *tall_pack), F32)],
    )
    res, *own = call(
        residual_kernel,
        [block, pack, pack],
        [sector_field, ready],
        micros=2,
    )
    nu_tall, main, nu_packs, main_side = call(
        operator_kernel,
        [padded, high, (4, *tall_pack), tall_pack],
        [nu, diag, *static, *ax, *own],
        micros=2,
        scratch=[pltpu.VMEM(tall_pack, F32)],
    )
    packs = [*own, *swapped(*own, SECTOR)]
    spread = (rows + 4 * per_pack, 2, width)
    ax = call(residual_edges_kernel, [spread, spread], [res, *packs])
    q, kq, sums = call(
        gram_kernel,
        [block, block, (1, width)],
        [res, *packs, *swapped(*ax, AXIAL), nu_tall, main, nu_packs, main_side],
        scratch=[pltpu.VMEM(padded, F32)] * 4 + [pltpu.VMEM((4, *tall_pack), F32)],
        micros=4,
    )
    sums = sums + lax.ppermute(sums, "core", [(0, 1), (1, 0)])
    chips = sectors * slabs // 2
    sums = jnp.broadcast_to(sums[None], (chips, 1, width))
    sums = lax.all_to_all(sums, ("chip", AXIAL), 0, 0)
    potential, misfit = call(final_kernel, [block, block], [sums.reshape(chips, width), v, res, q, kq])
    return relaxed, potential, misfit


def solution(mesh):
    thermal = P(SECTOR, AXIAL, None)
    magnetic = P(None, AXIAL, SECTOR)
    sectors, slabs = mesh.devices.shape
    cores = mesh.devices.reshape(sectors // 2, 2, slabs)
    return jax.shard_map(
        local,
        mesh=jax.sharding.Mesh(cores, (*SECTOR, AXIAL)),
        in_specs=(thermal,) * 3 + (magnetic,) * 6 + (P(),) * 3,
        out_specs=(thermal, magnetic, magnetic),
        check_vma=False,
    )
```
